32 devices in a mesh: groups: 2 (over x), dp: 16 (over z, y, core).
Axes of the slice: x: 2, y: 2, z: 4, core: 2. Of those that a mesh axis runs over, the one named last changes fastest.
Arguments:
- tokens: bfloat16 [16384, 1024], P(('groups', 'dp')), parts along dimension 0, may hold values from -8 to 8
- lengths: int32 [32, 8], P(('groups', 'dp')), parts along dimension 0, may hold values from 1 to 256, 512 in all within a row
- input_weight: bfloat16 [1024, 3072], P(None, 'dp'), may hold values from -0.5 to 0.5
- output_weight: bfloat16 [1024, 1024], P(None, 'dp'), may hold values from -0.1875 to 0.1875
- norm_gain: float32 [1024], replicated, may hold values from 0.25 to 1.75
- expand_weight: bfloat16 [1024, 2048], P(None, 'dp'), may hold values from -0.1875 to 0.1875
- shrink_weight: bfloat16 [2048, 1024], P(None, 'dp'), may hold values from -0.125 to 0.125
- assigned: int32 [16384], P(('groups', 'dp')), parts along dimension 0, may hold values from 0 to 63, as said below
- owner_map: int32 [128], P('groups'), parts along dimension 0, may hold values from 0 to 63, each once
- centroids: bfloat16 [64, 1024], P('dp'), may hold values from -3 to 3
Outputs:
- filed: bfloat16 [128, 256, 1024], P(('groups', 'dp')), parts along dimension 0
The draws below stay inside these ranges and needn't reach their ends.
There are 2 independent parts, one for each index of `groups`. The reference program is written for one: setup_inputs(seed, part) draws one part's arguments, and reference() takes and returns one part's arrays. A program takes and returns all parts, laid end to end along the dimension named above; an argument that names none is the same for every part. Nothing has to cross between parts.
Inputs may be any that keep to these rules, and one draw needn't show every extreme that they name: `assigned`: each device's 512 rows name no list more than 16 times, and one list is named exactly 16 times by the rows of every device. The 8 lengths of a device sum to 512; its passages lie end to end in its rows. `owner_map`: A permutation; the list with value p belongs to the device p // 4.
All inputs are finite; a program needn't handle non-finite values.
Results may differ from the reference program's by a relative error of at most 0.015.
Values may be sent and summed in bfloat16 or wider, within the bound.
No kernel may reach another device: no remote copies, remote signals or barrier semaphores. Data moves between devices by JAX's collectives and lax.ppermute only.
A program may use at most 128 MiB of HBM per device.

```python
import math
import jax
import jax.numpy as jnp
import numpy as np
from jax import lax

D = 1024
HEADS = 16
FF = 2048
TOK_DEV = 512
PASS_DEV = 8
MAXLEN = 256
NLIST = 64
SLOTS = 16
TOKENS = 8192
N_DP = 16


def draw_tokens(key, part):
    key = jax.random.fold_in(key, 5)
    first_key = jax.random.fold_in(key, 0)
    base = jax.random.normal(first_key, (TOKENS, D), jnp.float32)
    return jnp.clip(base, -6.0, 6.0).astype(jnp.bfloat16)


def draw_input_weight(key, part):
    key = jax.random.fold_in(key, 7)
    first_key, second_key, third_key = jax.random.split(key, 3)
    spread = D ** (-0.5)
    query_part = jax.random.normal(first_key, (D, D), jnp.float32) * spread
    other_part = jax.random.normal(second_key, (D, D), jnp.float32) * spread
    value_part = jax.random.normal(third_key, (D, D), jnp.float32) * spread
    joined = jnp.concatenate([query_part, other_part, value_part], axis=1)
    return jnp.clip(joined, -0.5, 0.5).astype(jnp.bfloat16)


def draw_assigned(key, part):
    key = jax.random.fold_in(key, 9)
    hot_key, block_key = jax.random.split(key)
    hot_list = jax.random.randint(hot_key, (), 0, NLIST)
    block_keys = jax.random.split(block_key, N_DP)

    def one_block(single_key):
        slot_key, order_key = jax.random.split(single_key)
        others = SLOTS + jax.random.permutation(slot_key, NLIST * SLOTS - SLOTS)
        picks = jnp.concatenate([jnp.arange(SLOTS, dtype=jnp.int32), others[:TOK_DEV - SLOTS].astype(jnp.int32)])
        chosen = (picks // SLOTS + hot_list) % NLIST
        order = jax.random.permutation(order_key, TOK_DEV)
        return chosen[order]
    return jax.vmap(one_block)(block_keys).reshape(TOKENS).astype(jnp.int32)


def block_scale(key, extent, cuts, low, high):
    def one(axis_at, shards_of):
        draws = jax.random.uniform(jax.random.fold_in(jax.random.fold_in(key, 6), axis_at), (shards_of,), jnp.float32, low / len(cuts), high / len(cuts))
        return jnp.repeat(jnp.exp(draws), extent[axis_at] // shards_of).reshape((-1,) + (1,) * (len(extent) - axis_at - 1))

    gain = one(*cuts[0])
    for cut in cuts[1:]:
        gain = gain * one(*cut)
    return gain


def split_up(count, total, most, skew):
    weights = [(1 << 20) // math.isqrt(standing ** skew) + 1 for standing in range(2, count + 1)]
    surplus, holding = total - most - (count - 1), [1] * (count - 1)
    while surplus > 0:
        free = [i for i in range(count - 1) if holding[i] < most]
        whole, budget = sum([weights[i] for i in free]), surplus
        for i in free:
            addition = min(most - holding[i], max(1, budget * weights[i] // whole), surplus)
            holding[i] = holding[i] + addition
            surplus = surplus - addition
    return np.array([most] + holding)


def ragged_sizes(stream_key, count, total, most, skew):
    if count == 2:
        one = jax.random.randint(stream_key, (), max(1, total - most), min(most, total - 1) + 1)
        return jnp.stack([one, total - one])
    sizes = jnp.asarray(split_up(count, total, most, skew), jnp.int32)
    twos = (count - 1) // 2
    source_of, taker = sizes[1:1 + 2 * twos:2], sizes[2:2 + 2 * twos:2]
    margin = jnp.minimum(source_of - 1, most - taker)
    shifted = jax.random.randint(jax.random.fold_in(stream_key, 1), (twos,), 0, 1 << 20) % (margin + 1)
    sizes = sizes.at[1:1 + 2 * twos:2].set(source_of - shifted).at[2:2 + 2 * twos:2].set(taker + shifted)
    return sizes[jax.random.permutation(jax.random.fold_in(stream_key, 2), count)]


def bell_draw(stream_key, extent, scale, bound, cuts=(), kind=jnp.bfloat16):
    loudness = block_scale(stream_key, extent, cuts, -0.22, 0.18) if cuts else 1.0
    values = jax.random.normal(stream_key, extent, jnp.float32) * scale * loudness
    return jnp.minimum(jnp.maximum(values, -bound), bound).astype(kind)


def setup_inputs(seed: int = 0, part: int = 0) -> dict:
    key_of = jax.random.split(jax.random.key(seed), 11)
    part_splits = jax.random.split(jax.random.fold_in(key_of[10], part), 11)
    return {
        "tokens": draw_tokens(jax.random.fold_in(jax.random.fold_in(key_of[10], part), 71), part),
        "lengths": jax.vmap(lambda own: ragged_sizes(own, PASS_DEV, TOK_DEV, MAXLEN, 2))(jax.random.split(part_splits[1], N_DP)).reshape((N_DP, PASS_DEV)).astype(jnp.int32),
        "input_weight": draw_input_weight(jax.random.fold_in(key_of[10], 71), part),
        "output_weight": bell_draw(key_of[3], (D, D), D ** -0.5, 0.1875, ((1, 16),)),
        "norm_gain": jnp.clip(1.0 + 0.15 * jax.random.normal(key_of[4], (D,), jnp.float32), 0.25, 1.75),
        "expand_weight": bell_draw(key_of[5], (D, FF), D ** -0.5, 0.1875, ((1, 16),)),
        "shrink_weight": bell_draw(key_of[6], (FF, D), FF ** -0.5, 0.125, ((1, 16),)),
        "assigned": draw_assigned(jax.random.fold_in(jax.random.fold_in(key_of[10], part), 71), part),
        "owner_map": jax.random.permutation(part_splits[8], NLIST).astype(jnp.int32),
        "centroids": bell_draw(key_of[9], (NLIST, D), 0.5, 3.0, ((0, 16),)),
    }


norm_eps = 1e-06
ridge_term = 0.05

def layer_norm(values, gain_row):
    row_mean = lax.optimization_barrier(jnp.mean(values, axis=-1, keepdims=True))
    centered = values - row_mean
    row_var = lax.optimization_barrier(jnp.mean(centered * centered, axis=-1, keepdims=True))
    return centered * lax.rsqrt(row_var + norm_eps) * gain_row

def segment_ids(length_row, row_count):
    boundary = jnp.cumsum(length_row).astype(jnp.int32)
    position = jnp.arange(row_count, dtype=jnp.int32)
    return lax.optimization_barrier(jnp.sum((position[:, None] >= boundary[None, :]).astype(jnp.int32), axis=1)).astype(jnp.int32)

def attend(queries, keys_in, values_in, length_row, head_count):
    row_count, model_width = queries.shape
    head_dim = model_width // head_count
    segment = segment_ids(length_row, row_count)
    same_passage = segment[:, None] == segment[None, :]
    score_scale = 1.0 / math.sqrt(head_dim)

    def split_heads(matrix):
        return matrix.reshape(row_count, head_count, head_dim).transpose(1, 0, 2)

    def one_head(head_parts):
        query_head, key_head, value_head = head_parts
        scores = jnp.dot(query_head.astype(jnp.float32), key_head.T.astype(jnp.float32), preferred_element_type=jnp.float32) * score_scale
        scores = jnp.where(same_passage, scores, -1e+30)
        weights = jax.nn.softmax(scores, axis=-1).astype(jnp.bfloat16)
        return jnp.dot(weights.astype(jnp.float32), value_head.astype(jnp.float32), preferred_element_type=jnp.float32).astype(jnp.bfloat16)
    mixed = lax.map(one_head, (split_heads(queries), split_heads(keys_in), split_heads(values_in)))
    return mixed.transpose(1, 0, 2).reshape(row_count, model_width)

def reference(tokens, lengths, input_weight, output_weight, norm_gain, expand_weight, shrink_weight, assigned, owner_map, centroids):
    total_rows, model_width = tokens.shape
    projected = jnp.dot(tokens.astype(jnp.float32), input_weight.astype(jnp.float32), preferred_element_type=jnp.float32).astype(jnp.bfloat16)

    def per_device(block_parts):
        query_block, key_block, value_block, length_row = block_parts
        return attend(query_block, key_block, value_block, length_row, HEADS)
    shaped = (N_DP, TOK_DEV, model_width)
    attended = lax.map(per_device, (projected[:, :model_width].reshape(shaped), projected[:, model_width:2 * model_width].reshape(shaped), projected[:, 2 * model_width:].reshape(shaped), lengths)).reshape(total_rows, model_width)
    mixed_out = jnp.dot(attended.astype(jnp.float32), output_weight.astype(jnp.float32), preferred_element_type=jnp.float32)
    first_norm = layer_norm(tokens.astype(jnp.float32) + mixed_out, norm_gain).astype(jnp.bfloat16)
    expanded = jax.nn.gelu(jnp.dot(first_norm.astype(jnp.float32), expand_weight.astype(jnp.float32), preferred_element_type=jnp.float32), approximate=False).astype(jnp.bfloat16)
    reduced = jnp.dot(expanded.astype(jnp.float32), shrink_weight.astype(jnp.float32), preferred_element_type=jnp.float32)
    embedded = layer_norm(first_norm.astype(jnp.float32) + reduced, 1.0).astype(jnp.bfloat16)
    gram = lax.dot_general(embedded.astype(jnp.float32), embedded.astype(jnp.float32), (((0,), (0,)), ((), ())), preferred_element_type=jnp.float32)
    covariance = gram / total_rows + ridge_term * jnp.eye(model_width, dtype=jnp.float32)
    factor = jnp.linalg.cholesky(covariance)
    whitened = jax.scipy.linalg.solve_triangular(factor, embedded.astype(jnp.float32).T, lower=True).T.astype(jnp.bfloat16)
    position = owner_map[assigned].astype(jnp.int32)
    choose = (assigned.reshape(N_DP, TOK_DEV)[:, :, None] == jnp.arange(NLIST, dtype=jnp.int32)[None, None, :]).astype(jnp.int32)
    earlier = (jnp.cumsum(choose, axis=1) - choose).astype(jnp.int32)
    rank_in_list = lax.optimization_barrier(jnp.sum(earlier * choose, axis=2)).astype(jnp.int32).reshape(total_rows)
    source = jnp.arange(total_rows, dtype=jnp.int32) // TOK_DEV
    slot_index = ((position * N_DP + source) * SLOTS + rank_in_list).astype(jnp.int32)
    residual = (whitened.astype(jnp.float32) - centroids[position].astype(jnp.float32)).astype(jnp.bfloat16)
    filed = jnp.zeros((NLIST * N_DP * SLOTS, model_width), jnp.bfloat16).at[slot_index].set(residual)
    return filed.reshape(NLIST, N_DP * SLOTS, model_width)
```

```python
import functools
import math

import jax
import jax.numpy as jnp
from jax import lax
from jax.experimental import pallas as pl
from jax.experimental.pallas import tpu as pltpu
from jax.sharding import PartitionSpec as P

HEADS = 16


norm_eps = 1e-06
ridge_term = 0.05


def layer_norm(values, gain_row):
    row_mean = jnp.mean(values, axis=-1, keepdims=True)
    centered = values - row_mean
    row_var = jnp.mean(centered * centered, axis=-1, keepdims=True)
    return centered * lax.rsqrt(row_var + norm_eps) * gain_row


def segment_ids(length_row, row_count):
    boundary = jnp.cumsum(length_row)
    position = jnp.arange(row_count, dtype=jnp.int32)
    return jnp.sum((position[:, None] >= boundary[None, :]).astype(jnp.int32), axis=1)


def attend(queries, keys_in, values_in, length_row, head_count):
    row_count, model_width = queries.shape
    head_dim = model_width // head_count
    segment = segment_ids(length_row, row_count)
    same_passage = segment[:, None] == segment[None, :]
    score_scale = 1.0 / math.sqrt(head_dim)

    def split_heads(matrix):
        return matrix.reshape(row_count, head_count, head_dim).transpose(1, 0, 2)

    def one_head(head_parts):
        query_head, key_head, value_head = head_parts
        scores = jnp.dot(query_head, key_head.T, preferred_element_type=jnp.float32) * score_scale
        scores = jnp.where(same_passage, scores, -1e30)
        weights = jax.nn.softmax(scores, axis=-1).astype(jnp.bfloat16)
        return jnp.dot(weights, value_head, preferred_element_type=jnp.float32).astype(jnp.bfloat16)

    mixed = lax.map(one_head, (split_heads(queries), split_heads(keys_in), split_heads(values_in)))
    return mixed.transpose(1, 0, 2).reshape(row_count, model_width)


BLOCK = 128
PANEL = 8


def split_bf16(value):
    high = value.astype(jnp.bfloat16)
    return high, (value - high.astype(jnp.float32)).astype(jnp.bfloat16)


def dot3(left, right, dims):
    lh, ll = left
    rh, rl = right
    dot = functools.partial(lax.dot_general, dimension_numbers=(dims, ((), ())), preferred_element_type=jnp.float32)
    return dot(lh, rh) + (dot(lh, rl) + dot(ll, rh))


def diagonal_inverse(rows):
    count = len(rows)
    lane = lax.broadcasted_iota(jnp.int32, (PANEL, BLOCK), 1)
    sub = lax.broadcasted_iota(jnp.int32, (PANEL, BLOCK), 0)
    shape = (PANEL, BLOCK)
    rows = list(rows)
    result = []
    for p in range(count):
        first = PANEL * p
        panel = rows[p]
        inside = (lane >= first) & (lane < first + PANEL)
        spread = [jnp.broadcast_to(panel[:, first + t : first + t + 1], shape) for t in range(PANEL)]
        entry = [[jnp.broadcast_to(spread[b][a : a + 1, :], shape) for b in range(a + 1)] for a in range(PANEL)]
        columns = [
            [jnp.broadcast_to(rows[i][:, first + t : first + t + 1], shape) for t in range(PANEL)]
            for i in range(p + 1, count)
        ]
        forward = [
            jnp.where(inside, jnp.where(lane == first + t, 1.0, 0.0), jnp.broadcast_to(panel[t : t + 1, :], shape))
            for t in range(PANEL)
        ]
        ratio = [[None] * PANEL for _ in range(PANEL)]
        kept = jnp.zeros(shape, jnp.float32)
        solved = [None] * PANEL
        for t in range(PANEL):
            root = lax.rsqrt(entry[t][t])
            inverse = root * root
            for a in range(t + 1, PANEL):
                ratio[a][t] = entry[a][t] * inverse
            for a in range(t + 1, PANEL):
                for b in range(t + 1, a + 1):
                    entry[a][b] = entry[a][b] - ratio[a][t] * entry[b][t]
            kept = jnp.where(sub == t, forward[t] * root, kept)
            solved[t] = forward[t] * inverse
            for a in range(t + 1, PANEL):
                forward[a] = forward[a] - ratio[a][t] * forward[t]
        for t in range(PANEL - 1, 0, -1):
            for a in range(t):
                solved[a] = solved[a] - ratio[t][a] * solved[t]
        result.append(jnp.where(lane <= first + sub, kept, 0.0))
        for i in range(p + 1, count):
            col = columns[i - p - 1]
            terms = [col[t] * solved[t] for t in range(PANEL)]
            while len(terms) > 1:
                terms = [a + b for a, b in zip(terms[::2], terms[1::2])]
            rows[i] = jnp.where(inside, 0.0, rows[i]) - terms[0]
    return result


def factor_kernel(scale, ridge, gram_ref, out_ref, work):
    width = gram_ref.shape[0]
    blocks = width // BLOCK
    eye = (
        lax.broadcasted_iota(jnp.int32, (BLOCK, BLOCK), 0) == lax.broadcasted_iota(jnp.int32, (BLOCK, BLOCK), 1)
    ).astype(jnp.float32)

    def load(i, carry):
        at = pl.ds(pl.multiple_of(i * BLOCK, BLOCK), BLOCK)
        work[at, :] = gram_ref[at, :] * scale
        work[at, at] = work[at, at] + ridge * eye
        return carry

    lax.fori_loop(0, blocks, load, 0)

    def step(j, carry):
        at = pl.ds(pl.multiple_of(j * BLOCK, BLOCK), BLOCK)
        diagonal = work[at, at]
        inverse = jnp.concatenate(
            diagonal_inverse([diagonal[PANEL * i : PANEL * (i + 1), :] for i in range(BLOCK // PANEL)]), axis=0
        )
        pair = split_bf16(inverse)
        work[at, at] = eye
        scaled = dot3(pair, split_bf16(work[at, :]), ((1,), (0,)))
        work[at, :] = scaled
        scaled_pair = split_bf16(scaled)

        def update(i, carry):
            here = pl.ds(pl.multiple_of(i * BLOCK, BLOCK), BLOCK)
            left = dot3(split_bf16(work[here, at]), pair, ((1,), (1,)))
            work[here, at] = jnp.zeros((BLOCK, BLOCK), jnp.float32)
            work[here, :] = work[here, :] - dot3(split_bf16(left), scaled_pair, ((1,), (0,)))
            return carry

        lax.fori_loop(j + 1, blocks, update, 0)
        column = lax.broadcasted_iota(jnp.int32, (BLOCK, width), 1)
        out_ref[at, :] = jnp.where(column < (j + 1) * BLOCK, scaled, 0.0).astype(out_ref.dtype)
        return carry

    lax.fori_loop(0, blocks, step, 0)


def inverse_factor(gram, scale, ridge):
    width = gram.shape[0]
    return pl.pallas_call(
        functools.partial(factor_kernel, scale, ridge),
        out_shape=jax.ShapeDtypeStruct((width, width), jnp.bfloat16),
        in_specs=[pl.BlockSpec(memory_space=pltpu.VMEM)],
        out_specs=pl.BlockSpec(memory_space=pltpu.VMEM),
        scratch_shapes=[pltpu.VMEM((width, width), jnp.float32)],
        compiler_params=pltpu.CompilerParams(vmem_limit_bytes=40 * 1024 * 1024),
    )(gram)


EMPTY = 64.0


def slots_of(assigned, owner_map, lists_owned, slot_count):
    row_count = assigned.shape[0]
    choose = assigned[:, None] == jnp.arange(owner_map.shape[0], dtype=jnp.int32)[None, :]
    position = jnp.sum(jnp.where(choose, owner_map[None, :], 0), axis=1)
    order = jnp.arange(row_count, dtype=jnp.int32)
    earlier = (assigned[:, None] == assigned[None, :]) & (order[:, None] > order[None, :])
    rank = jnp.sum(earlier.astype(jnp.int32), axis=1)
    return position * slot_count + rank


def place_rows(rows, slot_index, slot_total):
    chosen = jnp.arange(slot_total, dtype=jnp.int32)[:, None] == slot_index[None, :]
    placed = jnp.dot(chosen.astype(jnp.bfloat16), rows, preferred_element_type=jnp.float32)
    return jnp.where(jnp.any(chosen, axis=1, keepdims=True), placed, EMPTY).astype(jnp.bfloat16)


def body(
    tokens,
    lengths,
    input_weight,
    output_weight,
    norm_gain,
    expand_weight,
    shrink_weight,
    assigned,
    owner_map,
    centroids,
):
    row_count, model_width = tokens.shape
    device_count = lax.axis_size("dp")
    projected = jnp.dot(
        tokens,
        lax.all_gather(input_weight, "dp", axis=1, tiled=True),
        preferred_element_type=jnp.float32,
    ).astype(jnp.bfloat16)
    attended = attend(
        projected[:, :model_width],
        projected[:, model_width : 2 * model_width],
        projected[:, 2 * model_width :],
        lengths[0],
        HEADS,
    )
    mixed_out = jnp.dot(
        attended,
        lax.all_gather(output_weight, "dp", axis=1, tiled=True),
        preferred_element_type=jnp.float32,
    )
    first_norm = layer_norm(tokens.astype(jnp.float32) + mixed_out, norm_gain).astype(jnp.bfloat16)
    product = jnp.dot(
        first_norm,
        lax.all_gather(expand_weight, "dp", axis=1, tiled=True),
        preferred_element_type=jnp.float32,
    )
    expanded = jax.nn.gelu(product, approximate=False).astype(jnp.bfloat16)
    reduced = jnp.dot(
        expanded,
        lax.all_gather(shrink_weight, "dp", axis=1, tiled=True),
        preferred_element_type=jnp.float32,
    )
    embedded = layer_norm(first_norm.astype(jnp.float32) + reduced, 1.0).astype(jnp.bfloat16)
    lists_owned = centroids.shape[0]
    list_total = lists_owned * device_count
    slot_count = max(2, 2 * row_count // list_total)
    slot_index = slots_of(assigned, owner_map, lists_owned, slot_count)
    outgoing = place_rows(embedded, slot_index, list_total * slot_count)
    incoming = lax.all_to_all(
        outgoing.reshape(device_count, lists_owned, slot_count, model_width),
        "dp",
        split_axis=0,
        concat_axis=0,
        tiled=True,
    )
    gram = lax.dot_general(
        embedded, embedded, (((0,), (0,)), ((), ())), preferred_element_type=jnp.float32
    )
    total_gram = lax.psum(gram, "dp")
    inverse = inverse_factor(total_gram, 1.0 / (row_count * device_count), ridge_term)
    arrived = incoming.transpose(1, 0, 2, 3).reshape(-1, model_width)
    whitened = lax.dot_general(
        arrived, inverse, (((1,), (1,)), ((), ())), preferred_element_type=jnp.float32
    ).reshape(lists_owned, device_count * slot_count, model_width)
    occupied = arrived[:, :1].reshape(lists_owned, device_count * slot_count, 1) < EMPTY
    residual = whitened - centroids.astype(jnp.float32)[:, None, :]
    return jnp.where(occupied, residual, 0.0).astype(jnp.bfloat16)


def solution(mesh):
    in_specs = (
        P(("groups", "dp"), None),
        P(("groups", "dp"), None),
        P(None, "dp"),
        P(None, "dp"),
        P(),
        P(None, "dp"),
        P(None, "dp"),
        P(("groups", "dp")),
        P("groups"),
        P("dp", None),
    )
    out_specs = P(("groups", "dp"), None, None)
    return jax.shard_map(body, mesh=mesh, in_specs=in_specs, out_specs=out_specs, check_vma=False)
```

```python
import functools
import math

import jax
import jax.numpy as jnp
from jax import lax
from jax.experimental import pallas as pl
from jax.experimental.pallas import tpu as pltpu
from jax.sharding import PartitionSpec as P

HEADS = 16


norm_eps = 1e-06
ridge_term = 0.05


def layer_norm(values, gain_row):
    row_mean = jnp.mean(values, axis=-1, keepdims=True)
    centered = values - row_mean
    row_var = jnp.mean(centered * centered, axis=-1, keepdims=True)
    return centered * lax.rsqrt(row_var + norm_eps) * gain_row


def segment_ids(length_row, row_count):
    boundary = jnp.cumsum(length_row)
    position = jnp.arange(row_count, dtype=jnp.int32)
    return jnp.sum((position[:, None] >= boundary[None, :]).astype(jnp.int32), axis=1)


HEADS_STEP = 2


def attend_kernel(head_dim, column_ref, row_ref, query_ref, key_ref, value_ref, out_ref, bias):
    @pl.when(pl.program_id(0) == 0)
    def _():
        bias[...] = jnp.where(column_ref[...] == row_ref[...], 0.0, -1e30)

    score_scale = math.log2(math.e) / math.sqrt(head_dim)
    for head in range(HEADS_STEP):
        rows = slice(head * head_dim, (head + 1) * head_dim)
        scores = lax.dot_general(
            key_ref[rows, :], query_ref[rows, :], (((0,), (0,)), ((), ())), preferred_element_type=jnp.float32
        )
        scores = scores * score_scale + bias[...]
        weights = jnp.exp2(scores - jnp.max(scores, axis=0, keepdims=True))
        total = jnp.sum(weights, axis=0, keepdims=True)
        mixed = jnp.dot(value_ref[rows, :], weights.astype(jnp.bfloat16), preferred_element_type=jnp.float32)
        out_ref[rows, :] = (mixed * (1.0 / total)).astype(out_ref.dtype)


def attend(projected, segment):
    width, row_count = projected.shape[0] // 3, projected.shape[1]
    head_dim = width // HEADS
    block = (HEADS_STEP * head_dim, row_count)
    steps = HEADS // HEADS_STEP
    return pl.pallas_call(
        functools.partial(attend_kernel, head_dim),
        grid=(steps,),
        out_shape=jax.ShapeDtypeStruct((width, row_count), jnp.bfloat16),
        in_specs=[
            pl.BlockSpec((row_count, 1), lambda i: (0, 0)),
            pl.BlockSpec((1, row_count), lambda i: (0, 0)),
            pl.BlockSpec(block, lambda i: (i, 0)),
            pl.BlockSpec(block, lambda i: (i + steps, 0)),
            pl.BlockSpec(block, lambda i: (i + 2 * steps, 0)),
        ],
        out_specs=pl.BlockSpec(block, lambda i: (i, 0)),
        scratch_shapes=[pltpu.VMEM((row_count, row_count), jnp.float32)],
        compiler_params=pltpu.CompilerParams(vmem_limit_bytes=32 * 1024 * 1024),
        cost_estimate=pl.CostEstimate(
            flops=4 * HEADS * row_count * row_count * head_dim,
            bytes_accessed=8 * width * row_count,
            transcendentals=HEADS * row_count * row_count,
        ),
    )(segment[:, None], segment[None, :], projected, projected, projected)


def exchange(part, axis, bit):
    return lax.ppermute(part, axis, [(i, i ^ bit) for i in range(lax.axis_size(axis))])


def ordered(part, axis, bit):
    other = exchange(part, axis, bit)
    low = (lax.axis_index(axis) // bit) % 2 == 0
    return jnp.stack([jnp.where(low, part, other), jnp.where(low, other, part)])


def bits_of(size, least):
    bits = []
    while size // 2 >= least:
        size //= 2
        bits.append(size)
    return bits


def gather_rows(shard):
    groups, count = lax.axis_size("groups"), lax.axis_size("dp")
    rows, width = shard.shape
    unit = rows // groups // 2
    far, group_bits = bits_of(count, 4), bits_of(groups, 1)
    part = lax.dynamic_index_in_dim(shard.reshape(groups, 2, unit, width), lax.axis_index("groups"), 0, False)
    for bit in far:
        part = ordered(part, "dp", bit)
    part = part.reshape(-1, 2, unit, width)
    one, two = ordered(part[:, 0], "dp", 2), part[:, 1]
    for bit in group_bits:
        one, two = ordered(one, "groups", bit), ordered(two, "groups", bit)
    two = jnp.moveaxis(ordered(two, "dp", 2), 0, len(group_bits))
    whole = jnp.stack([ordered(one, "dp", 1), ordered(two, "dp", 1)])
    whole = whole.reshape((2,) * (3 + len(group_bits) + len(far)) + (unit, width))
    chip = 2 + len(group_bits)
    order = list(range(chip + len(far), chip, -1)) + [chip, 1] + list(range(chip - 1, 1, -1)) + [0]
    return whole.transpose(order + [chip + len(far) + 1, chip + len(far) + 2]).reshape(count * rows, width)


BLOCK = 128
PANEL = 8


def split_bf16(value):
    high = value.astype(jnp.bfloat16)
    return high, (value - high.astype(jnp.float32)).astype(jnp.bfloat16)


def dot3(left, right, dims):
    lh, ll = left
    rh, rl = right
    dot = functools.partial(lax.dot_general, dimension_numbers=(dims, ((), ())), preferred_element_type=jnp.float32)
    return dot(lh, rh) + (dot(lh, rl) + dot(ll, rh))


def diagonal_inverse(rows):
    count = len(rows)
    lane = lax.broadcasted_iota(jnp.int32, (PANEL, BLOCK), 1)
    sub = lax.broadcasted_iota(jnp.int32, (PANEL, BLOCK), 0)
    shape = (PANEL, BLOCK)
    rows = list(rows)
    result = []
    for p in range(count):
        first = PANEL * p
        panel = rows[p]
        inside = (lane >= first) & (lane < first + PANEL)
        spread = [jnp.broadcast_to(panel[:, first + t : first + t + 1], shape) for t in range(PANEL)]
        entry = [[jnp.broadcast_to(spread[b][a : a + 1, :], shape) for b in range(a + 1)] for a in range(PANEL)]
        columns = [
            [jnp.broadcast_to(rows[i][:, first + t : first + t + 1], shape) for t in range(PANEL)]
            for i in range(p + 1, count)
        ]
        forward = [
            jnp.where(inside, jnp.where(lane == first + t, 1.0, 0.0), jnp.broadcast_to(panel[t : t + 1, :], shape))
            for t in range(PANEL)
        ]
        ratio = [[None] * PANEL for _ in range(PANEL)]
        kept = jnp.zeros(shape, jnp.float32)
        solved = [None] * PANEL
        for t in range(PANEL):
            root = lax.rsqrt(entry[t][t])
            inverse = root * root
            for a in range(t + 1, PANEL):
                ratio[a][t] = entry[a][t] * inverse
            for a in range(t + 1, PANEL):
                for b in range(t + 1, a + 1):
                    entry[a][b] = entry[a][b] - ratio[a][t] * entry[b][t]
            kept = jnp.where(sub == t, forward[t] * root, kept)
            solved[t] = forward[t] * inverse
            for a in range(t + 1, PANEL):
                forward[a] = forward[a] - ratio[a][t] * forward[t]
        for t in range(PANEL - 1, 0, -1):
            for a in range(t):
                solved[a] = solved[a] - ratio[t][a] * solved[t]
        result.append(jnp.where(lane <= first + sub, kept, 0.0))
        for i in range(p + 1, count):
            col = columns[i - p - 1]
            terms = [col[t] * solved[t] for t in range(PANEL)]
            while len(terms) > 1:
                terms = [a + b for a, b in zip(terms[::2], terms[1::2])]
            rows[i] = jnp.where(inside, 0.0, rows[i]) - terms[0]
    return result


def factor_in_place(work):
    width = work.shape[0]
    blocks = width // BLOCK
    eye = identity(BLOCK)

    def step(j, carry):
        at = pl.ds(pl.multiple_of(j * BLOCK, BLOCK), BLOCK)
        diagonal = work[at, at]
        inverse = jnp.concatenate(
            diagonal_inverse([diagonal[PANEL * i : PANEL * (i + 1), :] for i in range(BLOCK // PANEL)]), axis=0
        )
        pair = split_bf16(inverse)
        work[at, at] = eye
        scaled = dot3(pair, split_bf16(work[at, :]), ((1,), (0,)))
        work[at, :] = scaled
        scaled_pair = split_bf16(scaled)

        def update(i, carry):
            here = pl.ds(pl.multiple_of(i * BLOCK, BLOCK), BLOCK)
            left = dot3(split_bf16(work[here, at]), pair, ((1,), (1,)))
            work[here, at] = jnp.zeros((BLOCK, BLOCK), jnp.float32)
            work[here, :] = work[here, :] - dot3(split_bf16(left), scaled_pair, ((1,), (0,)))
            return carry

        lax.fori_loop(j + 1, blocks, update, 0)
        return carry

    lax.fori_loop(0, blocks, step, 0)


def identity(size):
    return (
        lax.broadcasted_iota(jnp.int32, (size, size), 0) == lax.broadcasted_iota(jnp.int32, (size, size), 1)
    ).astype(jnp.float32)


def block_lower(value):
    row = lax.broadcasted_iota(jnp.int32, value.shape, 0) // BLOCK
    column = lax.broadcasted_iota(jnp.int32, value.shape, 1) // BLOCK
    return jnp.where(column <= row, value, 0.0)


def load_symmetric(tiles, scale, ridge, work):
    side = tiles[0].shape[0]
    diagonal = ridge * identity(side)
    low, high = slice(0, side), slice(side, 2 * side)
    work[low, low] = tiles[0][...] * scale + diagonal
    work[high, high] = tiles[1][...] * scale + diagonal
    cross = tiles[2][...] * scale
    work[high, low] = cross
    work[low, high] = cross.T


def first_kernel(scale, ridge, tiles_ref, out_ref, work):
    load_symmetric([tiles_ref.at[i] for i in range(3)], scale, ridge, work)
    factor_in_place(work)
    out_ref[...] = block_lower(work[...])


def second_kernel(scale, ridge, first_ref, tiles_ref, out_ref, work, under):
    half = first_ref.shape[0]
    side = half // 2
    load_symmetric([tiles_ref.at[4 + i] for i in range(3)], scale, ridge, work)
    first = split_bf16(first_ref[...])
    for i in range(2):
        rows = slice(i * side, (i + 1) * side)
        cross = jnp.concatenate([tiles_ref[2 * i], tiles_ref[2 * i + 1]], axis=1) * scale
        under[rows, :] = dot3(split_bf16(cross), first, ((1,), (1,)))
    pair = split_bf16(under[...])
    for i in range(2):
        rows = slice(i * side, (i + 1) * side)
        mine = tuple(part[rows, :] for part in pair)
        work[rows, :] = work[rows, :] - dot3(mine, pair, ((1,), (1,)))
    under[...] = dot3(pair, first, ((1,), (0,)))
    factor_in_place(work)
    second = block_lower(work[...])
    out_ref[:half, :half] = first_ref[...].astype(out_ref.dtype)
    out_ref[:half, half:] = jnp.zeros((half, half), out_ref.dtype)
    out_ref[half:, :half] = (-dot3(split_bf16(second), split_bf16(under[...]), ((1,), (0,)))).astype(out_ref.dtype)
    out_ref[half:, half:] = second.astype(out_ref.dtype)


def kernel_call(kernel, out, operands, scratch, cost):
    whole = pl.BlockSpec(memory_space=pltpu.VMEM)
    return pl.pallas_call(
        kernel,
        out_shape=out,
        in_specs=[whole] * len(operands),
        out_specs=whole,
        scratch_shapes=scratch,
        compiler_params=pltpu.CompilerParams(vmem_limit_bytes=40 * 1024 * 1024),
        cost_estimate=pl.CostEstimate(flops=cost, bytes_accessed=4 << 20, transcendentals=0),
    )(*operands)


CHAIN_FLOPS = 30_000_000_000


def inverse_first(tiles, scale, ridge):
    half = 2 * tiles.shape[-1]
    square = pltpu.VMEM((half, half), jnp.float32)
    return kernel_call(
        functools.partial(first_kernel, scale, ridge),
        jax.ShapeDtypeStruct((half, half), jnp.float32),
        (tiles,),
        [square],
        CHAIN_FLOPS,
    )


def inverse_second(first, tiles, scale, ridge):
    half = first.shape[0]
    square = pltpu.VMEM((half, half), jnp.float32)
    return kernel_call(
        functools.partial(second_kernel, scale, ridge),
        jax.ShapeDtypeStruct((2 * half, 2 * half), jnp.bfloat16),
        (first, tiles),
        [square, square],
        CHAIN_FLOPS,
    )


FIRST_TILES = ((0, 0), (1, 1), (1, 0))
SECOND_TILES = ((2, 0), (2, 1), (3, 0), (3, 1), (2, 2), (3, 3), (3, 2))


def gram_kernel(rows_ref, columns_ref, left_ref, right_ref, out_ref):
    out_ref[0] = lax.dot_general(
        left_ref[...], right_ref[...], (((0,), (0,)), ((), ())), preferred_element_type=jnp.float32
    )


def gram_tiles(values, tiles):
    count, width = values.shape
    side = width // 4
    rows = jnp.array([tile[0] for tile in tiles], jnp.int32)
    columns = jnp.array([tile[1] for tile in tiles], jnp.int32)
    return pl.pallas_call(
        gram_kernel,
        grid_spec=pltpu.PrefetchScalarGridSpec(
            num_scalar_prefetch=2,
            grid=(len(tiles),),
            in_specs=[
                pl.BlockSpec((count, side), lambda i, row, column: (0, row[i])),
                pl.BlockSpec((count, side), lambda i, row, column: (0, column[i])),
            ],
            out_specs=pl.BlockSpec((1, side, side), lambda i, row, column: (i, 0, 0)),
        ),
        out_shape=jax.ShapeDtypeStruct((len(tiles), side, side), jnp.float32),
        compiler_params=pltpu.CompilerParams(vmem_limit_bytes=24 * 1024 * 1024),
        cost_estimate=pl.CostEstimate(
            flops=2 * len(tiles) * count * side * side, bytes_accessed=4 << 20, transcendentals=0
        ),
    )(rows, columns, values, values)


def sum_tiles(tiles, whole_bits):
    part = tiles.reshape(-1, tiles.shape[-1])
    width = part.shape[1]
    bits = bits_of(lax.axis_size("dp"), 1)[::-1]
    near = bits[: len(bits) - whole_bits]
    for bit in near:
        halves = part.reshape(2, -1, width)
        high = (lax.axis_index("dp") // bit) % 2
        kept = lax.dynamic_index_in_dim(halves, high, 0, False)
        part = kept + exchange(lax.dynamic_index_in_dim(halves, 1 - high, 0, False), "dp", bit)
    for bit in bits[len(near) :]:
        part = part + exchange(part, "dp", bit)
    for bit in near[::-1]:
        part = ordered(part, "dp", bit).reshape(-1, width)
    return part.reshape(tiles.shape)


EMPTY = 64.0


def slots_of(assigned, owner_map, lists_owned, slot_count):
    row_count = assigned.shape[0]
    choose = assigned[:, None] == jnp.arange(owner_map.shape[0], dtype=jnp.int32)[None, :]
    position = jnp.sum(jnp.where(choose, owner_map[None, :], 0), axis=1)
    order = jnp.arange(row_count, dtype=jnp.int32)
    earlier = (assigned[:, None] == assigned[None, :]) & (order[:, None] > order[None, :])
    rank = jnp.sum(earlier.astype(jnp.int32), axis=1)
    return position * slot_count + rank


def place_rows(rows, slot_index, slot_total):
    chosen = jnp.arange(slot_total, dtype=jnp.int32)[:, None] == slot_index[None, :]
    placed = jnp.dot(chosen.astype(jnp.bfloat16), rows, preferred_element_type=jnp.float32)
    return jnp.where(jnp.any(chosen, axis=1, keepdims=True), placed, EMPTY).astype(jnp.bfloat16)


def body(
    tokens,
    lengths,
    input_weight,
    output_weight,
    norm_gain,
    expand_weight,
    shrink_weight,
    assigned,
    owner_map,
    centroids,
):
    row_count, model_width = tokens.shape
    device_count = lax.axis_size("dp")
    nt = functools.partial(
        lax.dot_general, dimension_numbers=(((1,), (1,)), ((), ())), preferred_element_type=jnp.float32
    )
    input_rows = gather_rows(input_weight.T)
    middle = jnp.concatenate([output_weight.T, expand_weight.T], axis=0)
    middle_rows = gather_rows(middle).reshape(device_count, -1, model_width)
    own_output = output_weight.shape[1]
    output_rows = middle_rows[:, :own_output].reshape(-1, model_width)
    expand_rows = middle_rows[:, own_output:].reshape(-1, model_width)
    shrink_rows = gather_rows(shrink_weight.T)
    projected = nt(input_rows, tokens).astype(jnp.bfloat16)
    attended = attend(projected, segment_ids(lengths[0], row_count))
    mixed_out = lax.dot_general(
        attended, output_rows, (((0,), (1,)), ((), ())), preferred_element_type=jnp.float32
    )
    first_norm = layer_norm(tokens.astype(jnp.float32) + mixed_out, norm_gain).astype(jnp.bfloat16)
    expanded = jax.nn.gelu(nt(first_norm, expand_rows), approximate=False).astype(jnp.bfloat16)
    reduced = nt(expanded, shrink_rows)
    embedded = layer_norm(first_norm.astype(jnp.float32) + reduced, 1.0).astype(jnp.bfloat16)
    lists_owned = centroids.shape[0]
    list_total = lists_owned * device_count
    slot_count = max(2, 2 * row_count // list_total)
    slot_index = slots_of(assigned, owner_map, lists_owned, slot_count)
    outgoing = place_rows(embedded, slot_index, list_total * slot_count)
    scale = 1.0 / (row_count * device_count)
    first_sum = sum_tiles(gram_tiles(embedded, FIRST_TILES), 2)
    second_sum = sum_tiles(gram_tiles(embedded, SECOND_TILES), 0)
    first = inverse_first(first_sum, scale, ridge_term)
    outgoing, second_sum = lax.optimization_barrier((outgoing, second_sum))
    incoming = lax.all_to_all(
        outgoing.reshape(device_count, lists_owned, slot_count, model_width),
        "dp",
        split_axis=0,
        concat_axis=0,
        tiled=True,
    )
    inverse = inverse_second(first, second_sum, scale, ridge_term)
    arrived = incoming.transpose(1, 0, 2, 3).reshape(-1, model_width)
    whitened = lax.dot_general(
        arrived, inverse, (((1,), (1,)), ((), ())), preferred_element_type=jnp.float32
    ).reshape(lists_owned, device_count * slot_count, model_width)
    occupied = arrived[:, :1].reshape(lists_owned, device_count * slot_count, 1) < EMPTY
    residual = whitened - centroids.astype(jnp.float32)[:, None, :]
    return jnp.where(occupied, residual, 0.0).astype(jnp.bfloat16)


def solution(mesh):
    in_specs = (
        P(("groups", "dp"), None),
        P(("groups", "dp"), None),
        P(None, "dp"),
        P(None, "dp"),
        P(),
        P(None, "dp"),
        P(None, "dp"),
        P(("groups", "dp")),
        P("groups"),
        P("dp", None),
    )
    out_specs = P(("groups", "dp"), None, None)
    return jax.shard_map(body, mesh=mesh, in_specs=in_specs, out_specs=out_specs, check_vma=False)
```

```python
import functools
import math

import jax
import jax.numpy as jnp
from jax import lax
from jax.experimental import pallas as pl
from jax.experimental.pallas import tpu as pltpu
from jax.sharding import PartitionSpec as P

HEADS = 16


norm_eps = 1e-06
ridge_term = 0.05


def layer_norm(values, gain_row):
    row_mean = jnp.mean(values, axis=-1, keepdims=True)
    centered = values - row_mean
    row_var = jnp.mean(centered * centered, axis=-1, keepdims=True)
    return centered * lax.rsqrt(row_var + norm_eps) * gain_row


def segment_ids(length_row, row_count):
    boundary = jnp.cumsum(length_row)
    position = jnp.arange(row_count, dtype=jnp.int32)
    return jnp.sum((position[:, None] >= boundary[None, :]).astype(jnp.int32), axis=1)


HEADS_STEP = 2


def attend_kernel(head_dim, column_ref, row_ref, query_ref, key_ref, value_ref, out_ref, bias):
    @pl.when(pl.program_id(0) == 0)
    def _():
        bias[...] = jnp.where(column_ref[...] == row_ref[...], 0.0, -1e30)

    score_scale = math.log2(math.e) / math.sqrt(head_dim)
    for head in range(HEADS_STEP):
        rows = slice(head * head_dim, (head + 1) * head_dim)
        scores = lax.dot_general(
            key_ref[rows, :], query_ref[rows, :], (((0,), (0,)), ((), ())), preferred_element_type=jnp.float32
        )
        scores = scores * score_scale + bias[...]
        weights = jnp.exp2(scores - jnp.max(scores, axis=0, keepdims=True))
        total = jnp.sum(weights, axis=0, keepdims=True)
        mixed = jnp.dot(value_ref[rows, :], weights.astype(jnp.bfloat16), preferred_element_type=jnp.float32)
        out_ref[rows, :] = (mixed * (1.0 / total)).astype(out_ref.dtype)


def attend(projected, segment):
    width, row_count = projected.shape[0] // 3, projected.shape[1]
    head_dim = width // HEADS
    block = (HEADS_STEP * head_dim, row_count)
    steps = HEADS // HEADS_STEP
    return pl.pallas_call(
        functools.partial(attend_kernel, head_dim),
        grid=(steps,),
        out_shape=jax.ShapeDtypeStruct((width, row_count), jnp.bfloat16),
        in_specs=[
            pl.BlockSpec((row_count, 1), lambda i: (0, 0)),
            pl.BlockSpec((1, row_count), lambda i: (0, 0)),
            pl.BlockSpec(block, lambda i: (i, 0)),
            pl.BlockSpec(block, lambda i: (i + steps, 0)),
            pl.BlockSpec(block, lambda i: (i + 2 * steps, 0)),
        ],
        out_specs=pl.BlockSpec(block, lambda i: (i, 0)),
        scratch_shapes=[pltpu.VMEM((row_count, row_count), jnp.float32)],
        compiler_params=pltpu.CompilerParams(vmem_limit_bytes=32 * 1024 * 1024),
        cost_estimate=pl.CostEstimate(
            flops=4 * HEADS * row_count * row_count * head_dim,
            bytes_accessed=8 * width * row_count,
            transcendentals=HEADS * row_count * row_count,
        ),
    )(segment[:, None], segment[None, :], projected, projected, projected)


def exchange(part, axis, bit):
    return lax.ppermute(part, axis, [(i, i ^ bit) for i in range(lax.axis_size(axis))])


def ordered(part, axis, bit, *beside):
    other = after(exchange(part, axis, bit), *beside)
    low = (lax.axis_index(axis) // bit) % 2 == 0
    return jnp.stack([jnp.where(low, part, other), jnp.where(low, other, part)])


def bits_of(size, least):
    bits = []
    while size // 2 >= least:
        size //= 2
        bits.append(size)
    return bits


def after(part, *earlier):
    return lax.optimization_barrier((part, *earlier))[0] if earlier else part


def own_share(shard):
    groups = lax.axis_size("groups")
    rows, width = shard.shape
    shares = shard.reshape(groups, 2, rows // groups // 2, width)
    return lax.dynamic_index_in_dim(shares, lax.axis_index("groups"), 0, False)


def gather_far(part, bits):
    tail = part.shape[-3:]
    for bit in bits:
        part = ordered(part, "dp", bit)
    return part.reshape((-1,) + tail)


def near_first(part, *beside):
    group_bit = bits_of(lax.axis_size("groups"), 1)[0]
    return ordered(part[:, 0], "dp", 2, *beside), ordered(part[:, 1], "groups", group_bit, *beside)


def near_rest(one, two, *beside):
    group_bits = bits_of(lax.axis_size("groups"), 1)
    for bit in group_bits:
        one = ordered(one, "groups", bit, *beside)
    for bit in group_bits[1:]:
        two = ordered(two, "groups", bit)
    return one, jnp.moveaxis(ordered(two, "dp", 2, *beside), 0, len(group_bits))


def gather_cores(one, two):
    unit, width = one.shape[-2:]
    count, groups = lax.axis_size("dp"), lax.axis_size("groups")
    far_bits, group_bits = len(bits_of(count, 4)), len(bits_of(groups, 1))
    whole = jnp.stack([ordered(one, "dp", 1), ordered(two, "dp", 1)])
    whole = whole.reshape((2,) * (3 + group_bits + far_bits) + (unit, width))
    chip = 2 + group_bits
    order = list(range(chip + far_bits, chip, -1)) + [chip, 1] + list(range(chip - 1, 1, -1)) + [0]
    whole = whole.transpose(order + [chip + far_bits + 1, chip + far_bits + 2])
    return whole.reshape(count * groups * 2 * unit, width)


BLOCK = 128
PANEL = 8


def split_bf16(value):
    high = value.astype(jnp.bfloat16)
    return high, (value - high.astype(jnp.float32)).astype(jnp.bfloat16)


def dot3(left, right, dims):
    lh, ll = left
    rh, rl = right
    dot = functools.partial(lax.dot_general, dimension_numbers=(dims, ((), ())), preferred_element_type=jnp.float32)
    return dot(lh, rh) + (dot(lh, rl) + dot(ll, rh))


def diagonal_inverse(rows):
    count = len(rows)
    lane = lax.broadcasted_iota(jnp.int32, (PANEL, BLOCK), 1)
    sub = lax.broadcasted_iota(jnp.int32, (PANEL, BLOCK), 0)
    shape = (PANEL, BLOCK)
    rows = list(rows)
    result = []
    for p in range(count):
        first = PANEL * p
        panel = rows[p]
        inside = (lane >= first) & (lane < first + PANEL)
        spread = [jnp.broadcast_to(panel[:, first + t : first + t + 1], shape) for t in range(PANEL)]
        entry = [[jnp.broadcast_to(spread[b][a : a + 1, :], shape) for b in range(a + 1)] for a in range(PANEL)]
        columns = [
            [jnp.broadcast_to(rows[i][:, first + t : first + t + 1], shape) for t in range(PANEL)]
            for i in range(p + 1, count)
        ]
        forward = [
            jnp.where(inside, jnp.where(lane == first + t, 1.0, 0.0), jnp.broadcast_to(panel[t : t + 1, :], shape))
            for t in range(PANEL)
        ]
        ratio = [[None] * PANEL for _ in range(PANEL)]
        kept = jnp.zeros(shape, jnp.float32)
        solved = [None] * PANEL
        for t in range(PANEL):
            root = lax.rsqrt(entry[t][t])
            inverse = root * root
            for a in range(t + 1, PANEL):
                ratio[a][t] = entry[a][t] * inverse
            for a in range(t + 1, PANEL):
                for b in range(t + 1, a + 1):
                    entry[a][b] = entry[a][b] - ratio[a][t] * entry[b][t]
            kept = jnp.where(sub == t, forward[t] * root, kept)
            solved[t] = forward[t] * inverse
            for a in range(t + 1, PANEL):
                forward[a] = forward[a] - ratio[a][t] * forward[t]
        for t in range(PANEL - 1, 0, -1):
            for a in range(t):
                solved[a] = solved[a] - ratio[t][a] * solved[t]
        result.append(jnp.where(lane <= first + sub, kept, 0.0))
        for i in range(p + 1, count):
            col = columns[i - p - 1]
            terms = [col[t] * solved[t] for t in range(PANEL)]
            while len(terms) > 1:
                terms = [a + b for a, b in zip(terms[::2], terms[1::2])]
            rows[i] = jnp.where(inside, 0.0, rows[i]) - terms[0]
    return result


def factor_step(work, j):
    blocks = work.shape[0] // BLOCK
    at = slice(j * BLOCK, (j + 1) * BLOCK)
    diagonal = work[at, at]
    inverse = jnp.concatenate(
        diagonal_inverse([diagonal[PANEL * i : PANEL * (i + 1), :] for i in range(BLOCK // PANEL)]), axis=0
    )
    pair = split_bf16(inverse)
    work[at, at] = identity(BLOCK)
    scaled = dot3(pair, split_bf16(work[at, :]), ((1,), (0,)))
    work[at, :] = scaled
    if j + 1 == blocks:
        return
    scaled_pair = split_bf16(scaled)
    below = slice((j + 1) * BLOCK, blocks * BLOCK)
    left = dot3(split_bf16(work[below, at]), pair, ((1,), (1,)))
    work[below, at] = jnp.zeros((left.shape[0], BLOCK), jnp.float32)
    work[below, :] = work[below, :] - dot3(split_bf16(left), scaled_pair, ((1,), (0,)))


def factor_in_place(work):
    for j in range(work.shape[0] // BLOCK):
        factor_step(work, j)


def identity(size):
    return (
        lax.broadcasted_iota(jnp.int32, (size, size), 0) == lax.broadcasted_iota(jnp.int32, (size, size), 1)
    ).astype(jnp.float32)


def block_lower(value):
    row = lax.broadcasted_iota(jnp.int32, value.shape, 0) // BLOCK
    column = lax.broadcasted_iota(jnp.int32, value.shape, 1) // BLOCK
    return jnp.where(column <= row, value, 0.0)


def load_symmetric(tiles, scale, ridge, work):
    side = tiles[0].shape[0]
    diagonal = ridge * identity(side)
    low, high = slice(0, side), slice(side, 2 * side)
    work[low, low] = tiles[0][...] * scale + diagonal
    work[high, high] = tiles[1][...] * scale + diagonal
    cross = tiles[2][...] * scale
    work[high, low] = cross
    work[low, high] = cross.T


def first_kernel(scale, ridge, tiles_ref, out_ref):
    load_symmetric([tiles_ref.at[i] for i in range(3)], scale, ridge, out_ref)
    factor_step(out_ref, 0)


def later_kernel(j, work_ref, out_ref):
    out_ref[...] = work_ref[...]
    factor_step(out_ref, j)
    if (j + 1) * BLOCK == out_ref.shape[0]:
        out_ref[...] = block_lower(out_ref[...])


def second_kernel(scale, ridge, first_ref, tiles_ref, out_ref, work, under):
    half = first_ref.shape[0]
    side = half // 2
    load_symmetric([tiles_ref.at[4 + i] for i in range(3)], scale, ridge, work)
    first = split_bf16(first_ref[...])
    for i in range(2):
        rows = slice(i * side, (i + 1) * side)
        cross = jnp.concatenate([tiles_ref[2 * i], tiles_ref[2 * i + 1]], axis=1) * scale
        under[rows, :] = dot3(split_bf16(cross), first, ((1,), (1,)))
    pair = split_bf16(under[...])
    for i in range(2):
        rows = slice(i * side, (i + 1) * side)
        mine = tuple(part[rows, :] for part in pair)
        work[rows, :] = work[rows, :] - dot3(mine, pair, ((1,), (1,)))
    under[...] = dot3(pair, first, ((1,), (0,)))
    factor_in_place(work)
    second = block_lower(work[...])
    out_ref[:half, :half] = first_ref[...].astype(out_ref.dtype)
    out_ref[:half, half:] = jnp.zeros((half, half), out_ref.dtype)
    out_ref[half:, :half] = (-dot3(split_bf16(second), split_bf16(under[...]), ((1,), (0,)))).astype(out_ref.dtype)
    out_ref[half:, half:] = second.astype(out_ref.dtype)


def kernel_call(kernel, out, operands, scratch, cost):
    whole = pl.BlockSpec(memory_space=pltpu.VMEM)
    return pl.pallas_call(
        kernel,
        out_shape=out,
        in_specs=[whole] * len(operands),
        out_specs=whole,
        scratch_shapes=scratch,
        compiler_params=pltpu.CompilerParams(vmem_limit_bytes=40 * 1024 * 1024),
        cost_estimate=pl.CostEstimate(flops=cost, bytes_accessed=4 << 20, transcendentals=0),
    )(*operands)


CHAIN_FLOPS = 30_000_000_000


def inverse_first(tiles, scale, ridge):
    half = 2 * tiles.shape[-1]
    shape = jax.ShapeDtypeStruct((half, half), jnp.float32)
    steps = half // BLOCK
    stages = [
        kernel_call(functools.partial(first_kernel, scale, ridge), shape, (tiles,), [], CHAIN_FLOPS // steps)
    ]
    for j in range(1, steps):
        stages.append(
            kernel_call(functools.partial(later_kernel, j), shape, (stages[-1],), [], CHAIN_FLOPS // steps)
        )
    return stages


def inverse_second(first, tiles, scale, ridge):
    half = first.shape[0]
    square = pltpu.VMEM((half, half), jnp.float32)
    return kernel_call(
        functools.partial(second_kernel, scale, ridge),
        jax.ShapeDtypeStruct((2 * half, 2 * half), jnp.bfloat16),
        (first, tiles),
        [square, square],
        CHAIN_FLOPS,
    )


FIRST_TILES = ((0, 0), (1, 1), (1, 0))
SECOND_TILES = ((2, 0), (2, 1), (3, 0), (3, 1), (2, 2), (3, 3), (3, 2))


def gram_kernel(rows_ref, columns_ref, left_ref, right_ref, out_ref):
    out_ref[0] = lax.dot_general(
        left_ref[...], right_ref[...], (((0,), (0,)), ((), ())), preferred_element_type=jnp.float32
    )


def gram_tiles(values, tiles):
    count, width = values.shape
    side = width // 4
    rows = jnp.array([tile[0] for tile in tiles], jnp.int32)
    columns = jnp.array([tile[1] for tile in tiles], jnp.int32)
    return pl.pallas_call(
        gram_kernel,
        grid_spec=pltpu.PrefetchScalarGridSpec(
            num_scalar_prefetch=2,
            grid=(len(tiles),),
            in_specs=[
                pl.BlockSpec((count, side), lambda i, row, column: (0, row[i])),
                pl.BlockSpec((count, side), lambda i, row, column: (0, column[i])),
            ],
            out_specs=pl.BlockSpec((1, side, side), lambda i, row, column: (i, 0, 0)),
        ),
        out_shape=jax.ShapeDtypeStruct((len(tiles), side, side), jnp.float32),
        compiler_params=pltpu.CompilerParams(vmem_limit_bytes=24 * 1024 * 1024),
        cost_estimate=pl.CostEstimate(
            flops=2 * len(tiles) * count * side * side, bytes_accessed=4 << 20, transcendentals=0
        ),
    )(rows, columns, values, values)


def halve(part, bit, start=(), beside=()):
    halves = part.reshape(2, -1, part.shape[-1])
    high = (lax.axis_index("dp") // bit) % 2
    kept = lax.dynamic_index_in_dim(halves, high, 0, False)
    sent = after(lax.dynamic_index_in_dim(halves, 1 - high, 0, False), *start)
    return kept + after(exchange(sent, "dp", bit), *beside)


def rejoin(part, bit, *beside):
    return ordered(part, "dp", bit, *beside).reshape(-1, part.shape[-1])


def sum_first(part):
    bits = bits_of(lax.axis_size("dp"), 1)[::-1]
    stages = [part]
    for bit in bits[:-2]:
        stages.append(halve(stages[-1], bit))
    for bit in bits[-2:]:
        stages.append(stages[-1] + exchange(stages[-1], "dp", bit))
    for bit in bits[:-2][::-1]:
        stages.append(rejoin(stages[-1], bit))
    return stages[1:]


def sum_second(part, sums, factors):
    bits = bits_of(lax.axis_size("dp"), 1)[::-1]
    gaps = [sums[k + (k >= len(bits) - 2)] for k in range(len(bits))] + [factors[0]]
    for k, bit in enumerate(bits):
        part = halve(part, bit, (gaps[k],), (gaps[k + 1],))
    for k, bit in enumerate(bits[::-1]):
        if bit == 2:
            near = part
        part = rejoin(part, bit, factors[min(k + 1, len(factors) - 1)])
    return part, near


def filing_kernel(rows_ref, inverse_ref, centroids_ref, out_ref):
    count, _, slots, width = rows_ref.shape
    rows = rows_ref[...].reshape(count * slots, width)
    whitened = lax.dot_general(rows, inverse_ref[...], (((1,), (1,)), ((), ())), preferred_element_type=jnp.float32)
    residual = whitened - centroids_ref[0].astype(jnp.float32)
    out_ref[0] = jnp.where(rows[:, :1].astype(jnp.float32) < EMPTY, residual, 0.0).astype(out_ref.dtype)


def file_rows(incoming, inverse, centroids):
    count, lists, slots, width = incoming.shape
    return pl.pallas_call(
        filing_kernel,
        grid=(lists,),
        in_specs=[
            pl.BlockSpec((count, 1, slots, width), lambda i: (0, i, 0, 0)),
            pl.BlockSpec((width, width), lambda i: (0, 0)),
            pl.BlockSpec((1, 1, width), lambda i: (i, 0, 0)),
        ],
        out_specs=pl.BlockSpec((1, count * slots, width), lambda i: (i, 0, 0)),
        out_shape=jax.ShapeDtypeStruct((lists, count * slots, width), jnp.bfloat16),
        compiler_params=pltpu.CompilerParams(vmem_limit_bytes=24 * 1024 * 1024),
    )(incoming, inverse, centroids[:, None, :])


EMPTY = 64.0


def slots_of(assigned, owner_map, lists_owned, slot_count):
    row_count = assigned.shape[0]
    choose = assigned[:, None] == jnp.arange(owner_map.shape[0], dtype=jnp.int32)[None, :]
    position = jnp.sum(jnp.where(choose, owner_map[None, :], 0), axis=1)
    order = jnp.arange(row_count, dtype=jnp.int32)
    earlier = (assigned[:, None] == assigned[None, :]) & (order[:, None] > order[None, :])
    rank = jnp.sum(earlier.astype(jnp.int32), axis=1)
    return position * slot_count + rank


def place_rows(rows, slot_index, slot_total):
    chosen = jnp.arange(slot_total, dtype=jnp.int32)[:, None] == slot_index[None, :]
    placed = jnp.dot(chosen.astype(jnp.bfloat16), rows, preferred_element_type=jnp.float32)
    return jnp.where(jnp.any(chosen, axis=1, keepdims=True), placed, EMPTY).astype(jnp.bfloat16)


def body(
    tokens,
    lengths,
    input_weight,
    output_weight,
    norm_gain,
    expand_weight,
    shrink_weight,
    assigned,
    owner_map,
    centroids,
):
    row_count, model_width = tokens.shape
    device_count = lax.axis_size("dp")
    nt = functools.partial(
        lax.dot_general, dimension_numbers=(((1,), (1,)), ((), ())), preferred_element_type=jnp.float32
    )
    middle = jnp.concatenate([output_weight.T, expand_weight.T], axis=0)
    far_bits = bits_of(device_count, 4)
    near, far = far_bits[1:], far_bits[:1]
    input_part = gather_far(gather_far(own_share(input_weight.T), far), near)
    middle_part = gather_far(after(own_share(middle), input_part), far)
    input_part = near_first(input_part)
    middle_part = gather_far(after(middle_part, *input_part), near)
    input_part = near_rest(*input_part)
    shrink_part = gather_far(after(own_share(shrink_weight.T), *input_part), far)
    middle_part = near_first(after(middle_part, *input_part))
    projected = nt(gather_cores(*input_part), tokens).astype(jnp.bfloat16)
    shrink_part = gather_far(after(shrink_part, *middle_part), near)
    attended = attend(after(projected, *middle_part), segment_ids(lengths[0], row_count))
    middle_part = near_rest(*middle_part, attended)
    middle_rows = gather_cores(*middle_part).reshape(device_count, -1, model_width)
    own_output = output_weight.shape[1]
    output_rows = middle_rows[:, :own_output].reshape(-1, model_width)
    expand_rows = middle_rows[:, own_output:].reshape(-1, model_width)
    mixed_out = lax.dot_general(
        attended, output_rows, (((0,), (1,)), ((), ())), preferred_element_type=jnp.float32
    )
    first_norm = layer_norm(tokens.astype(jnp.float32) + mixed_out, norm_gain).astype(jnp.bfloat16)
    shrink_part = near_first(after(shrink_part, *middle_part), first_norm)
    expanded = jax.nn.gelu(nt(after(first_norm, *shrink_part), expand_rows), approximate=False).astype(jnp.bfloat16)
    shrink_part = near_rest(*shrink_part, expanded)
    shrink_rows = gather_cores(*shrink_part)
    reduced = nt(expanded, shrink_rows)
    embedded = layer_norm(first_norm.astype(jnp.float32) + reduced, 1.0).astype(jnp.bfloat16)
    lists_owned = centroids.shape[0]
    list_total = lists_owned * device_count
    slot_count = max(2, 2 * row_count // list_total)
    slot_index = slots_of(assigned, owner_map, lists_owned, slot_count)
    outgoing = place_rows(embedded, slot_index, list_total * slot_count)
    scale = 1.0 / (row_count * device_count)
    first_tiles = gram_tiles(embedded, FIRST_TILES)
    second_tiles = gram_tiles(after(embedded, first_tiles), SECOND_TILES)
    sums = sum_first(first_tiles.reshape(-1, first_tiles.shape[-1]))
    stages = inverse_first(sums[-1].reshape(first_tiles.shape), scale, ridge_term)
    second_sum, near = sum_second(second_tiles.reshape(-1, second_tiles.shape[-1]), sums, stages)
    second_sum = second_sum.reshape(second_tiles.shape)
    first = stages[-1]
    outgoing = after(outgoing, near)
    incoming = lax.all_to_all(
        outgoing.reshape(device_count, lists_owned, slot_count, model_width),
        "dp",
        split_axis=0,
        concat_axis=0,
        tiled=True,
    )
    inverse = inverse_second(first, second_sum, scale, ridge_term)
    if slot_count % 16 == 0:
        return file_rows(incoming, inverse, centroids)
    arrived = incoming.transpose(1, 0, 2, 3).reshape(-1, model_width)
    whitened = lax.dot_general(
        arrived, inverse, (((1,), (1,)), ((), ())), preferred_element_type=jnp.float32
    ).reshape(lists_owned, device_count * slot_count, model_width)
    occupied = arrived[:, :1].reshape(lists_owned, device_count * slot_count, 1) < EMPTY
    residual = whitened - centroids.astype(jnp.float32)[:, None, :]
    return jnp.where(occupied, residual, 0.0).astype(jnp.bfloat16)


def solution(mesh):
    in_specs = (
        P(("groups", "dp"), None),
        P(("groups", "dp"), None),
        P(None, "dp"),
        P(None, "dp"),
        P(),
        P(None, "dp"),
        P(None, "dp"),
        P(("groups", "dp")),
        P("groups"),
        P("dp", None),
    )
    out_specs = P(("groups", "dp"), None, None)
    return jax.shard_map(body, mesh=mesh, in_specs=in_specs, out_specs=out_specs, check_vma=False)
```

```python
import functools
import math

import jax
import jax.numpy as jnp
from jax import lax
from jax.experimental import pallas as pl
from jax.experimental.pallas import tpu as pltpu
from jax.sharding import PartitionSpec as P

HEADS = 16


norm_eps = 1e-06
ridge_term = 0.05


def layer_norm(values, gain_row):
    row_mean = jnp.mean(values, axis=-1, keepdims=True)
    centered = values - row_mean
    row_var = jnp.mean(centered * centered, axis=-1, keepdims=True)
    return centered * lax.rsqrt(row_var + norm_eps) * gain_row


def segment_ids(length_row, row_count):
    boundary = jnp.cumsum(length_row)
    position = jnp.arange(row_count, dtype=jnp.int32)
    return jnp.sum((position[:, None] >= boundary[None, :]).astype(jnp.int32), axis=1)


HEADS_STEP = 2


def attend_kernel(head_dim, column_ref, row_ref, query_ref, key_ref, value_ref, out_ref, bias):
    @pl.when(pl.program_id(0) == 0)
    def _():
        bias[...] = jnp.where(column_ref[...] == row_ref[...], 0.0, -1e30)

    score_scale = math.log2(math.e) / math.sqrt(head_dim)
    for head in range(HEADS_STEP):
        rows = slice(head * head_dim, (head + 1) * head_dim)
        scores = lax.dot_general(
            key_ref[rows, :], query_ref[rows, :], (((0,), (0,)), ((), ())), preferred_element_type=jnp.float32
        )
        scores = scores * score_scale + bias[...]
        weights = jnp.exp2(scores - jnp.max(scores, axis=0, keepdims=True))
        total = jnp.sum(weights, axis=0, keepdims=True)
        mixed = jnp.dot(value_ref[rows, :], weights.astype(jnp.bfloat16), preferred_element_type=jnp.float32)
        out_ref[rows, :] = (mixed * (1.0 / total)).astype(out_ref.dtype)


def attend(projected, segment):
    width, row_count = projected.shape[0] // 3, projected.shape[1]
    head_dim = width // HEADS
    block = (HEADS_STEP * head_dim, row_count)
    steps = HEADS // HEADS_STEP
    return pl.pallas_call(
        functools.partial(attend_kernel, head_dim),
        grid=(steps,),
        out_shape=jax.ShapeDtypeStruct((width, row_count), jnp.bfloat16),
        in_specs=[
            pl.BlockSpec((row_count, 1), lambda i: (0, 0)),
            pl.BlockSpec((1, row_count), lambda i: (0, 0)),
            pl.BlockSpec(block, lambda i: (i, 0)),
            pl.BlockSpec(block, lambda i: (i + steps, 0)),
            pl.BlockSpec(block, lambda i: (i + 2 * steps, 0)),
        ],
        out_specs=pl.BlockSpec(block, lambda i: (i, 0)),
        scratch_shapes=[pltpu.VMEM((row_count, row_count), jnp.float32)],
        compiler_params=pltpu.CompilerParams(vmem_limit_bytes=32 * 1024 * 1024),
        cost_estimate=pl.CostEstimate(
            flops=4 * HEADS * row_count * row_count * head_dim,
            bytes_accessed=8 * width * row_count,
            transcendentals=HEADS * row_count * row_count,
        ),
    )(segment[:, None], segment[None, :], projected, projected, projected)


ERF_SHIFT = 0.3275911
ERF_TERMS = (1.061405429, -1.453152027, 1.421413741, -0.284496736, 0.254829592)


def gelu(value):
    reach = jnp.abs(value) * math.sqrt(0.5)
    below = 1.0 + ERF_SHIFT * reach
    t = pl.reciprocal(below, approx=True)
    t = t * (2.0 - below * t)
    poly = ERF_TERMS[0]
    for term in ERF_TERMS[1:]:
        poly = poly * t + term
    tail = 0.5 * value * (poly * t * jnp.exp2(reach * reach * -math.log2(math.e)))
    return jnp.where(value < 0.0, tail, value - tail)


def expand_kernel(rows_ref, weight_ref, out_ref):
    product = lax.dot_general(
        rows_ref[...], weight_ref[...], (((1,), (1,)), ((), ())), preferred_element_type=jnp.float32
    )
    out_ref[...] = gelu(product).astype(out_ref.dtype)


def expand(rows, weight):
    count, width = rows.shape
    hidden = weight.shape[0]
    tile = 256
    return pl.pallas_call(
        expand_kernel,
        grid=(hidden // tile,),
        in_specs=[
            pl.BlockSpec((count, width), lambda i: (0, 0)),
            pl.BlockSpec((tile, width), lambda i: (i, 0)),
        ],
        out_specs=pl.BlockSpec((count, tile), lambda i: (0, i)),
        out_shape=jax.ShapeDtypeStruct((count, hidden), jnp.bfloat16),
        compiler_params=pltpu.CompilerParams(vmem_limit_bytes=24 * 1024 * 1024),
        cost_estimate=pl.CostEstimate(
            flops=8 * count * width * hidden, bytes_accessed=8 << 20, transcendentals=2 * count * hidden
        ),
    )(rows, weight)


def exchange(part, axis, bit):
    return lax.ppermute(part, axis, [(i, i ^ bit) for i in range(lax.axis_size(axis))])


def ordered(part, axis, bit, *beside):
    other = after(exchange(part, axis, bit), *beside)
    low = (lax.axis_index(axis) // bit) % 2 == 0
    return jnp.stack([jnp.where(low, part, other), jnp.where(low, other, part)])


def bits_of(size, least):
    bits = []
    while size // 2 >= least:
        size //= 2
        bits.append(size)
    return bits


def after(part, *earlier):
    return lax.optimization_barrier((part, *earlier))[0] if earlier else part


def own_share(shard):
    groups = lax.axis_size("groups")
    rows, width = shard.shape
    shares = shard.reshape(groups, 2, rows // groups // 2, width)
    return lax.dynamic_index_in_dim(shares, lax.axis_index("groups"), 0, False)


def gather_far(part, bits, *beside):
    tail = part.shape[-3:]
    for bit in bits:
        part = ordered(part, "dp", bit, *beside)
    return part.reshape((-1,) + tail)


def near_first(part, *beside):
    group_bit = bits_of(lax.axis_size("groups"), 1)[0]
    return ordered(part[:, 0], "dp", 2, *beside), ordered(part[:, 1], "groups", group_bit, *beside)


def near_rest(one, two, *beside):
    group_bits = bits_of(lax.axis_size("groups"), 1)
    for bit in group_bits:
        one = ordered(one, "groups", bit, *beside)
    for bit in group_bits[1:]:
        two = ordered(two, "groups", bit)
    return one, jnp.moveaxis(ordered(two, "dp", 2, *beside), 0, len(group_bits))


def gather_cores(one, two):
    unit, width = one.shape[-2:]
    count, groups = lax.axis_size("dp"), lax.axis_size("groups")
    far_bits, group_bits = len(bits_of(count, 4)), len(bits_of(groups, 1))
    whole = jnp.stack([ordered(one, "dp", 1), ordered(two, "dp", 1)])
    whole = whole.reshape((2,) * (3 + group_bits + far_bits) + (unit, width))
    chip = 2 + group_bits
    order = list(range(chip + far_bits, chip, -1)) + [chip, 1] + list(range(chip - 1, 1, -1)) + [0]
    whole = whole.transpose(order + [chip + far_bits + 1, chip + far_bits + 2])
    return whole.reshape(count * groups * 2 * unit, width)


BLOCK = 128
PANEL = 8


def split_bf16(value):
    high = value.astype(jnp.bfloat16)
    return high, (value - high.astype(jnp.float32)).astype(jnp.bfloat16)


def dot3(left, right, dims):
    lh, ll = left
    rh, rl = right
    dot = functools.partial(lax.dot_general, dimension_numbers=(dims, ((), ())), preferred_element_type=jnp.float32)
    return dot(lh, rh) + (dot(lh, rl) + dot(ll, rh))


def diagonal_inverse(rows):
    count = len(rows)
    lane = lax.broadcasted_iota(jnp.int32, (PANEL, BLOCK), 1)
    sub = lax.broadcasted_iota(jnp.int32, (PANEL, BLOCK), 0)
    shape = (PANEL, BLOCK)
    rows = list(rows)
    result = []
    for p in range(count):
        first = PANEL * p
        panel = rows[p]
        inside = (lane >= first) & (lane < first + PANEL)
        spread = [jnp.broadcast_to(panel[:, first + t : first + t + 1], shape) for t in range(PANEL)]
        entry = [[jnp.broadcast_to(spread[b][a : a + 1, :], shape) for b in range(a + 1)] for a in range(PANEL)]
        columns = [
            [jnp.broadcast_to(rows[i][:, first + t : first + t + 1], shape) for t in range(PANEL)]
            for i in range(p + 1, count)
        ]
        forward = [
            jnp.where(inside, jnp.where(lane == first + t, 1.0, 0.0), jnp.broadcast_to(panel[t : t + 1, :], shape))
            for t in range(PANEL)
        ]
        ratio = [[None] * PANEL for _ in range(PANEL)]
        kept = jnp.zeros(shape, jnp.float32)
        solved = [None] * PANEL
        for t in range(PANEL):
            root = lax.rsqrt(entry[t][t])
            inverse = root * root
            for a in range(t + 1, PANEL):
                ratio[a][t] = entry[a][t] * inverse
            for a in range(t + 1, PANEL):
                for b in range(t + 1, a + 1):
                    entry[a][b] = entry[a][b] - ratio[a][t] * entry[b][t]
            kept = jnp.where(sub == t, forward[t] * root, kept)
            solved[t] = forward[t] * inverse
            for a in range(t + 1, PANEL):
                forward[a] = forward[a] - ratio[a][t] * forward[t]
        for t in range(PANEL - 1, 0, -1):
            for a in range(t):
                solved[a] = solved[a] - ratio[t][a] * solved[t]
        result.append(jnp.where(lane <= first + sub, kept, 0.0))
        for i in range(p + 1, count):
            col = columns[i - p - 1]
            terms = [col[t] * solved[t] for t in range(PANEL)]
            while len(terms) > 1:
                terms = [a + b for a, b in zip(terms[::2], terms[1::2])]
            rows[i] = jnp.where(inside, 0.0, rows[i]) - terms[0]
    return result


def factor_step(work, j):
    blocks = work.shape[0] // BLOCK
    at = slice(j * BLOCK, (j + 1) * BLOCK)
    diagonal = work[at, at]
    inverse = jnp.concatenate(
        diagonal_inverse([diagonal[PANEL * i : PANEL * (i + 1), :] for i in range(BLOCK // PANEL)]), axis=0
    )
    pair = split_bf16(inverse)
    work[at, at] = identity(BLOCK)
    scaled = dot3(pair, split_bf16(work[at, :]), ((1,), (0,)))
    work[at, :] = scaled
    if j + 1 == blocks:
        return
    scaled_pair = split_bf16(scaled)
    below = slice((j + 1) * BLOCK, blocks * BLOCK)
    left = dot3(split_bf16(work[below, at]), pair, ((1,), (1,)))
    work[below, at] = jnp.zeros((left.shape[0], BLOCK), jnp.float32)
    work[below, :] = work[below, :] - dot3(split_bf16(left), scaled_pair, ((1,), (0,)))


def factor_in_place(work):
    for j in range(work.shape[0] // BLOCK):
        factor_step(work, j)


def identity(size):
    return (
        lax.broadcasted_iota(jnp.int32, (size, size), 0) == lax.broadcasted_iota(jnp.int32, (size, size), 1)
    ).astype(jnp.float32)


def block_lower(value):
    row = lax.broadcasted_iota(jnp.int32, value.shape, 0) // BLOCK
    column = lax.broadcasted_iota(jnp.int32, value.shape, 1) // BLOCK
    return jnp.where(column <= row, value, 0.0)


def load_symmetric(tiles, scale, ridge, work):
    side = tiles[0].shape[0]
    diagonal = ridge * identity(side)
    low, high = slice(0, side), slice(side, 2 * side)
    work[low, low] = tiles[0][...] * scale + diagonal
    work[high, high] = tiles[1][...] * scale + diagonal
    cross = tiles[2][...] * scale
    work[high, low] = cross
    work[low, high] = cross.T


def first_kernel(scale, ridge, tiles_ref, out_ref):
    load_symmetric([tiles_ref.at[i] for i in range(3)], scale, ridge, out_ref)
    factor_step(out_ref, 0)


def later_kernel(j, work_ref, out_ref):
    out_ref[...] = work_ref[...]
    factor_step(out_ref, j)
    if (j + 1) * BLOCK == out_ref.shape[0]:
        out_ref[...] = block_lower(out_ref[...])


def second_kernel(scale, ridge, first_ref, tiles_ref, out_ref, work, under):
    half = first_ref.shape[0]
    side = half // 2
    load_symmetric([tiles_ref.at[4 + i] for i in range(3)], scale, ridge, work)
    first = split_bf16(first_ref[...])
    for i in range(2):
        rows = slice(i * side, (i + 1) * side)
        cross = jnp.concatenate([tiles_ref[2 * i], tiles_ref[2 * i + 1]], axis=1) * scale
        under[rows, :] = dot3(split_bf16(cross), first, ((1,), (1,)))
    pair = split_bf16(under[...])
    for i in range(2):
        rows = slice(i * side, (i + 1) * side)
        mine = tuple(part[rows, :] for part in pair)
        work[rows, :] = work[rows, :] - dot3(mine, pair, ((1,), (1,)))
    under[...] = dot3(pair, first, ((1,), (0,)))
    factor_in_place(work)
    second = block_lower(work[...])
    out_ref[:half, :half] = first_ref[...].astype(out_ref.dtype)
    out_ref[:half, half:] = jnp.zeros((half, half), out_ref.dtype)
    out_ref[half:, :half] = (-dot3(split_bf16(second), split_bf16(under[...]), ((1,), (0,)))).astype(out_ref.dtype)
    out_ref[half:, half:] = second.astype(out_ref.dtype)


def kernel_call(kernel, out, operands, scratch, cost):
    whole = pl.BlockSpec(memory_space=pltpu.VMEM)
    return pl.pallas_call(
        kernel,
        out_shape=out,
        in_specs=[whole] * len(operands),
        out_specs=whole,
        scratch_shapes=scratch,
        compiler_params=pltpu.CompilerParams(vmem_limit_bytes=40 * 1024 * 1024),
        cost_estimate=pl.CostEstimate(flops=cost, bytes_accessed=4 << 20, transcendentals=0),
    )(*operands)


CHAIN_FLOPS = 30_000_000_000


def inverse_first(tiles, scale, ridge):
    half = 2 * tiles.shape[-1]
    shape = jax.ShapeDtypeStruct((half, half), jnp.float32)
    steps = half // BLOCK
    stages = [
        kernel_call(functools.partial(first_kernel, scale, ridge), shape, (tiles,), [], CHAIN_FLOPS // steps)
    ]
    for j in range(1, steps):
        stages.append(
            kernel_call(functools.partial(later_kernel, j), shape, (stages[-1],), [], CHAIN_FLOPS // steps)
        )
    return stages


def inverse_second(first, tiles, scale, ridge):
    half = first.shape[0]
    square = pltpu.VMEM((half, half), jnp.float32)
    return kernel_call(
        functools.partial(second_kernel, scale, ridge),
        jax.ShapeDtypeStruct((2 * half, 2 * half), jnp.bfloat16),
        (first, tiles),
        [square, square],
        CHAIN_FLOPS,
    )


FIRST_TILES = ((0, 0), (1, 1), (1, 0))
SECOND_TILES = ((2, 0), (2, 1), (3, 0), (3, 1), (2, 2), (3, 3), (3, 2))


def gram_kernel(rows_ref, columns_ref, left_ref, right_ref, out_ref):
    out_ref[0] = lax.dot_general(
        left_ref[...], right_ref[...], (((0,), (0,)), ((), ())), preferred_element_type=jnp.float32
    )


def gram_tiles(values, tiles):
    count, width = values.shape
    side = width // 4
    rows = jnp.array([tile[0] for tile in tiles], jnp.int32)
    columns = jnp.array([tile[1] for tile in tiles], jnp.int32)
    return pl.pallas_call(
        gram_kernel,
        grid_spec=pltpu.PrefetchScalarGridSpec(
            num_scalar_prefetch=2,
            grid=(len(tiles),),
            in_specs=[
                pl.BlockSpec((count, side), lambda i, row, column: (0, row[i])),
                pl.BlockSpec((count, side), lambda i, row, column: (0, column[i])),
            ],
            out_specs=pl.BlockSpec((1, side, side), lambda i, row, column: (i, 0, 0)),
        ),
        out_shape=jax.ShapeDtypeStruct((len(tiles), side, side), jnp.float32),
        compiler_params=pltpu.CompilerParams(vmem_limit_bytes=24 * 1024 * 1024),
        cost_estimate=pl.CostEstimate(
            flops=2 * len(tiles) * count * side * side, bytes_accessed=4 << 20, transcendentals=0
        ),
    )(rows, columns, values, values)


def halve(part, bit, start=(), beside=()):
    halves = part.reshape(2, -1, part.shape[-1])
    high = (lax.axis_index("dp") // bit) % 2
    kept = lax.dynamic_index_in_dim(halves, high, 0, False)
    sent = after(lax.dynamic_index_in_dim(halves, 1 - high, 0, False), *start)
    return kept + after(exchange(sent, "dp", bit), *beside)


def rejoin(part, bit, *beside):
    return ordered(part, "dp", bit, *beside).reshape(-1, part.shape[-1])


def sum_both(first, second):
    bits = bits_of(lax.axis_size("dp"), 1)[::-1]
    near, far = bits[:-2], bits[-2:]
    first = halve(first, near[0])
    second_sent = after(second, first)
    for bit in near[1:]:
        first = halve(first, bit)
    second = halve(second_sent, bits[0], (), (first,))
    first = first + after(exchange(first, "dp", far[0]), second)
    second_next = functools.partial(halve, second, bits[1])
    first = first + exchange(first, "dp", far[1])
    second = second_next((), (first,))
    first = rejoin(first, near[-1], second)
    for bit in near[:-1][::-1]:
        first = rejoin(first, bit)

    def rest(besides, outgoing):
        part, at = second, 0
        for bit in bits[2:]:
            part = halve(part, bit, (), besides[at : at + 1])
            at += 1
        for bit in bits[::-1]:
            if bit == 2:
                outgoing = after(outgoing, part)
                part = rejoin(part, bit, outgoing)
            else:
                part = rejoin(part, bit, *besides[at : at + 1])
            at += 1
        return part, outgoing

    return first, rest


def filing_kernel(rows_ref, inverse_ref, centroids_ref, out_ref):
    count, _, slots, width = rows_ref.shape
    rows = rows_ref[...].reshape(count * slots, width)
    whitened = lax.dot_general(rows, inverse_ref[...], (((1,), (1,)), ((), ())), preferred_element_type=jnp.float32)
    residual = whitened - centroids_ref[0].astype(jnp.float32)
    out_ref[0] = jnp.where(rows[:, :1].astype(jnp.float32) < EMPTY, residual, 0.0).astype(out_ref.dtype)


def file_rows(incoming, inverse, centroids):
    count, lists, slots, width = incoming.shape
    return pl.pallas_call(
        filing_kernel,
        grid=(lists,),
        in_specs=[
            pl.BlockSpec((count, 1, slots, width), lambda i: (0, i, 0, 0)),
            pl.BlockSpec((width, width), lambda i: (0, 0)),
            pl.BlockSpec((1, 1, width), lambda i: (i, 0, 0)),
        ],
        out_specs=pl.BlockSpec((1, count * slots, width), lambda i: (i, 0, 0)),
        out_shape=jax.ShapeDtypeStruct((lists, count * slots, width), jnp.bfloat16),
        compiler_params=pltpu.CompilerParams(vmem_limit_bytes=24 * 1024 * 1024),
    )(incoming, inverse, centroids[:, None, :])


EMPTY = 64.0


def slots_of(assigned, owner_map, lists_owned, slot_count):
    row_count = assigned.shape[0]
    choose = assigned[:, None] == jnp.arange(owner_map.shape[0], dtype=jnp.int32)[None, :]
    position = jnp.sum(jnp.where(choose, owner_map[None, :], 0), axis=1)
    order = jnp.arange(row_count, dtype=jnp.int32)
    earlier = (assigned[:, None] == assigned[None, :]) & (order[:, None] > order[None, :])
    rank = jnp.sum(earlier.astype(jnp.int32), axis=1)
    return position * slot_count + rank


def place_rows(rows, slot_index, slot_total):
    chosen = jnp.arange(slot_total, dtype=jnp.int32)[:, None] == slot_index[None, :]
    placed = jnp.dot(chosen.astype(jnp.bfloat16), rows, preferred_element_type=jnp.float32)
    return jnp.where(jnp.any(chosen, axis=1, keepdims=True), placed, EMPTY).astype(jnp.bfloat16)


def body(
    tokens,
    lengths,
    input_weight,
    output_weight,
    norm_gain,
    expand_weight,
    shrink_weight,
    assigned,
    owner_map,
    centroids,
):
    row_count, model_width = tokens.shape
    device_count = lax.axis_size("dp")
    nt = functools.partial(
        lax.dot_general, dimension_numbers=(((1,), (1,)), ((), ())), preferred_element_type=jnp.float32
    )
    middle = jnp.concatenate([output_weight.T, expand_weight.T], axis=0)
    far_bits = bits_of(device_count, 4)
    near, far = far_bits[1:], far_bits[:1]
    input_part = gather_far(gather_far(own_share(input_weight.T), far), near)
    middle_part = gather_far(after(own_share(middle), input_part), far)
    input_first = near_first(input_part)
    middle_part = gather_far(middle_part, near, *input_first)
    shrink_part = gather_far(after(own_share(shrink_weight.T), middle_part), far)
    input_part = near_rest(*input_first)
    middle_first = near_first(middle_part, *input_part)
    shrink_part = gather_far(shrink_part, near, *input_part)
    projected = nt(gather_cores(*input_part), tokens).astype(jnp.bfloat16)
    attended = attend(after(projected, *middle_first), segment_ids(lengths[0], row_count))
    middle_part = near_rest(*middle_first, attended)
    shrink_first = near_first(after(shrink_part, *middle_first), attended)
    middle_rows = gather_cores(*middle_part).reshape(device_count, -1, model_width)
    own_output = output_weight.shape[1]
    output_rows = middle_rows[:, :own_output].reshape(-1, model_width)
    expand_rows = middle_rows[:, own_output:].reshape(-1, model_width)
    mixed_out = lax.dot_general(
        attended, output_rows, (((0,), (1,)), ((), ())), preferred_element_type=jnp.float32
    )
    first_norm = layer_norm(tokens.astype(jnp.float32) + mixed_out, norm_gain).astype(jnp.bfloat16)
    expanded = expand(after(first_norm, *shrink_first), expand_rows)
    shrink_part = near_rest(*shrink_first, expanded)
    shrink_rows = gather_cores(*shrink_part)
    reduced = nt(expanded, shrink_rows)
    embedded = layer_norm(first_norm.astype(jnp.float32) + reduced, 1.0).astype(jnp.bfloat16)
    lists_owned = centroids.shape[0]
    list_total = lists_owned * device_count
    slot_count = max(2, 2 * row_count // list_total)
    slot_index = slots_of(assigned, owner_map, lists_owned, slot_count)
    outgoing = place_rows(embedded, slot_index, list_total * slot_count)
    scale = 1.0 / (row_count * device_count)
    first_tiles = gram_tiles(embedded, FIRST_TILES)
    second_tiles = gram_tiles(after(embedded, first_tiles), SECOND_TILES)
    flat = functools.partial(jnp.reshape, shape=(-1, first_tiles.shape[-1]))
    first_sum, rest = sum_both(flat(first_tiles), flat(second_tiles))
    stages = inverse_first(first_sum.reshape(first_tiles.shape), scale, ridge_term)
    second_sum, outgoing = rest(stages, outgoing)
    second_sum = second_sum.reshape(second_tiles.shape)
    first = stages[-1]
    incoming = lax.all_to_all(
        outgoing.reshape(device_count, lists_owned, slot_count, model_width),
        "dp",
        split_axis=0,
        concat_axis=0,
        tiled=True,
    )
    inverse = inverse_second(first, second_sum, scale, ridge_term)
    if slot_count % 16 == 0:
        return file_rows(incoming, inverse, centroids)
    arrived = incoming.transpose(1, 0, 2, 3).reshape(-1, model_width)
    whitened = lax.dot_general(
        arrived, inverse, (((1,), (1,)), ((), ())), preferred_element_type=jnp.float32
    ).reshape(lists_owned, device_count * slot_count, model_width)
    occupied = arrived[:, :1].reshape(lists_owned, device_count * slot_count, 1) < EMPTY
    residual = whitened - centroids.astype(jnp.float32)[:, None, :]
    return jnp.where(occupied, residual, 0.0).astype(jnp.bfloat16)


def solution(mesh):
    in_specs = (
        P(("groups", "dp"), None),
        P(("groups", "dp"), None),
        P(None, "dp"),
        P(None, "dp"),
        P(),
        P(None, "dp"),
        P(None, "dp"),
        P(("groups", "dp")),
        P("groups"),
        P("dp", None),
    )
    out_specs = P(("groups", "dp"), None, None)
    return jax.shard_map(body, mesh=mesh, in_specs=in_specs, out_specs=out_specs, check_vma=False)
```

```python
import functools
import math

import jax
import jax.numpy as jnp
from jax import lax
from jax.experimental import pallas as pl
from jax.experimental.pallas import tpu as pltpu
from jax.sharding import PartitionSpec as P

HEADS = 16


norm_eps = 1e-06
ridge_term = 0.05


def layer_norm(values, gain_row):
    row_mean = jnp.mean(values, axis=-1, keepdims=True)
    centered = values - row_mean
    row_var = jnp.mean(centered * centered, axis=-1, keepdims=True)
    return centered * lax.rsqrt(row_var + norm_eps) * gain_row


def segment_ids(length_row, row_count):
    boundary = jnp.cumsum(length_row)
    position = jnp.arange(row_count, dtype=jnp.int32)
    return jnp.sum((position[:, None] >= boundary[None, :]).astype(jnp.int32), axis=1)


HEADS_STEP = 2


def attend_kernel(head_dim, column_ref, row_ref, query_ref, key_ref, value_ref, out_ref, bias):
    @pl.when(pl.program_id(0) == 0)
    def _():
        bias[...] = jnp.where(column_ref[...] == row_ref[...], 0.0, -1e30)

    score_scale = math.log2(math.e) / math.sqrt(head_dim)
    for head in range(HEADS_STEP):
        rows = slice(head * head_dim, (head + 1) * head_dim)
        scores = lax.dot_general(
            key_ref[rows, :], query_ref[rows, :], (((0,), (0,)), ((), ())), preferred_element_type=jnp.float32
        )
        scores = scores * score_scale + bias[...]
        weights = jnp.exp2(scores - jnp.max(scores, axis=0, keepdims=True))
        total = jnp.sum(weights, axis=0, keepdims=True)
        mixed = jnp.dot(value_ref[rows, :], weights.astype(jnp.bfloat16), preferred_element_type=jnp.float32)
        out_ref[rows, :] = (mixed * (1.0 / total)).astype(out_ref.dtype)


def attend(projected, segment):
    width, row_count = projected.shape[0] // 3, projected.shape[1]
    head_dim = width // HEADS
    block = (HEADS_STEP * head_dim, row_count)
    steps = HEADS // HEADS_STEP
    return pl.pallas_call(
        functools.partial(attend_kernel, head_dim),
        grid=(steps,),
        out_shape=jax.ShapeDtypeStruct((width, row_count), jnp.bfloat16),
        in_specs=[
            pl.BlockSpec((row_count, 1), lambda i: (0, 0)),
            pl.BlockSpec((1, row_count), lambda i: (0, 0)),
            pl.BlockSpec(block, lambda i: (i, 0)),
            pl.BlockSpec(block, lambda i: (i + steps, 0)),
            pl.BlockSpec(block, lambda i: (i + 2 * steps, 0)),
        ],
        out_specs=pl.BlockSpec(block, lambda i: (i, 0)),
        scratch_shapes=[pltpu.VMEM((row_count, row_count), jnp.float32)],
        compiler_params=pltpu.CompilerParams(vmem_limit_bytes=32 * 1024 * 1024),
        cost_estimate=pl.CostEstimate(
            flops=4 * HEADS * row_count * row_count * head_dim,
            bytes_accessed=8 * width * row_count,
            transcendentals=HEADS * row_count * row_count,
        ),
    )(segment[:, None], segment[None, :], projected, projected, projected)


ERF_SHIFT = 0.3275911
ERF_TERMS = (1.061405429, -1.453152027, 1.421413741, -0.284496736, 0.254829592)


def gelu(value):
    reach = jnp.abs(value) * math.sqrt(0.5)
    below = 1.0 + ERF_SHIFT * reach
    t = pl.reciprocal(below, approx=True)
    t = t * (2.0 - below * t)
    poly = ERF_TERMS[0]
    for term in ERF_TERMS[1:]:
        poly = poly * t + term
    tail = 0.5 * value * (poly * t * jnp.exp2(reach * reach * -math.log2(math.e)))
    return jnp.where(value < 0.0, tail, value - tail)


def expand_kernel(rows_ref, weight_ref, out_ref):
    product = lax.dot_general(
        rows_ref[...], weight_ref[...], (((1,), (1,)), ((), ())), preferred_element_type=jnp.float32
    )
    out_ref[...] = gelu(product).astype(out_ref.dtype)


def expand(rows, weight):
    count, width = rows.shape
    hidden = weight.shape[0]
    tile = 256
    return pl.pallas_call(
        expand_kernel,
        grid=(hidden // tile,),
        in_specs=[
            pl.BlockSpec((count, width), lambda i: (0, 0)),
            pl.BlockSpec((tile, width), lambda i: (i, 0)),
        ],
        out_specs=pl.BlockSpec((count, tile), lambda i: (0, i)),
        out_shape=jax.ShapeDtypeStruct((count, hidden), jnp.bfloat16),
        compiler_params=pltpu.CompilerParams(vmem_limit_bytes=24 * 1024 * 1024),
        cost_estimate=pl.CostEstimate(
            flops=8 * count * width * hidden, bytes_accessed=8 << 20, transcendentals=2 * count * hidden
        ),
    )(rows, weight)


def exchange(part, axis, bit):
    return lax.ppermute(part, axis, [(i, i ^ bit) for i in range(lax.axis_size(axis))])


def ordered(part, axis, bit, *beside):
    other = after(exchange(part, axis, bit), *beside)
    low = (lax.axis_index(axis) // bit) % 2 == 0
    return jnp.stack([jnp.where(low, part, other), jnp.where(low, other, part)])


def bits_of(size, least):
    bits = []
    while size // 2 >= least:
        size //= 2
        bits.append(size)
    return bits


def after(part, *earlier):
    return lax.optimization_barrier((part, *earlier))[0] if earlier else part


def own_share(shard):
    groups = lax.axis_size("groups")
    rows, width = shard.shape
    shares = shard.reshape(groups, 2, rows // groups // 2, width)
    return lax.dynamic_index_in_dim(shares, lax.axis_index("groups"), 0, False)


def gather_far(part, bits, *beside):
    tail = part.shape[-3:]
    for bit in bits:
        part = ordered(part, "dp", bit, *beside)
    return part.reshape((-1,) + tail)


def near_first(part, *beside):
    group_bit = bits_of(lax.axis_size("groups"), 1)[0]
    return ordered(part[:, 0], "dp", 2, *beside), ordered(part[:, 1], "groups", group_bit, *beside)


def near_rest(one, two, *beside):
    group_bits = bits_of(lax.axis_size("groups"), 1)
    for bit in group_bits:
        one = ordered(one, "groups", bit, *beside)
    for bit in group_bits[1:]:
        two = ordered(two, "groups", bit)
    return one, jnp.moveaxis(ordered(two, "dp", 2, *beside), 0, len(group_bits))


def gather_cores(one, two):
    unit, width = one.shape[-2:]
    count, groups = lax.axis_size("dp"), lax.axis_size("groups")
    far_bits, group_bits = len(bits_of(count, 4)), len(bits_of(groups, 1))
    whole = jnp.stack([ordered(one, "dp", 1), ordered(two, "dp", 1)])
    whole = whole.reshape((2,) * (3 + group_bits + far_bits) + (unit, width))
    chip = 2 + group_bits
    order = list(range(chip + far_bits, chip, -1)) + [chip, 1] + list(range(chip - 1, 1, -1)) + [0]
    whole = whole.transpose(order + [chip + far_bits + 1, chip + far_bits + 2])
    return whole.reshape(count * groups * 2 * unit, width)


BLOCK = 128
PANEL = 8


def split_bf16(value):
    high = value.astype(jnp.bfloat16)
    return high, (value - high.astype(jnp.float32)).astype(jnp.bfloat16)


def dot3(left, right, dims):
    lh, ll = left
    rh, rl = right
    dot = functools.partial(lax.dot_general, dimension_numbers=(dims, ((), ())), preferred_element_type=jnp.float32)
    return dot(lh, rh) + (dot(lh, rl) + dot(ll, rh))


def diagonal_inverse(rows):
    count = len(rows)
    lane = lax.broadcasted_iota(jnp.int32, (PANEL, BLOCK), 1)
    sub = lax.broadcasted_iota(jnp.int32, (PANEL, BLOCK), 0)
    shape = (PANEL, BLOCK)
    rows = list(rows)
    result = []
    for p in range(count):
        first = PANEL * p
        panel = rows[p]
        inside = (lane >= first) & (lane < first + PANEL)
        spread = [jnp.broadcast_to(panel[:, first + t : first + t + 1], shape) for t in range(PANEL)]
        entry = [[jnp.broadcast_to(spread[b][a : a + 1, :], shape) for b in range(a + 1)] for a in range(PANEL)]
        columns = [
            [jnp.broadcast_to(rows[i][:, first + t : first + t + 1], shape) for t in range(PANEL)]
            for i in range(p + 1, count)
        ]
        forward = [
            jnp.where(inside, jnp.where(lane == first + t, 1.0, 0.0), jnp.broadcast_to(panel[t : t + 1, :], shape))
            for t in range(PANEL)
        ]
        ahead = columns[0] if p + 1 < count else None
        moved = jnp.where(inside, 0.0, rows[p + 1]) if p + 1 < count else None
        ratio = [[None] * PANEL for _ in range(PANEL)]
        kept = jnp.zeros(shape, jnp.float32)
        solved = [None] * PANEL
        for t in range(PANEL):
            root = lax.rsqrt(entry[t][t])
            inverse = root * root
            for a in range(t + 1, PANEL):
                ratio[a][t] = entry[a][t] * inverse
            for a in range(t + 1, PANEL):
                for b in range(t + 1, a + 1):
                    entry[a][b] = entry[a][b] - (entry[a][t] * entry[b][t]) * inverse
            kept = jnp.where(sub == t, forward[t] * root, kept)
            solved[t] = forward[t] * inverse
            if ahead is not None:
                moved = moved - ahead[t] * solved[t]
                ahead = ahead[: t + 1] + [ahead[a] - ratio[a][t] * ahead[t] for a in range(t + 1, PANEL)]
            for a in range(t + 1, PANEL):
                forward[a] = forward[a] - ratio[a][t] * forward[t]
        for t in range(PANEL - 1, 0, -1):
            for a in range(t):
                solved[a] = solved[a] - ratio[t][a] * solved[t]
        result.append(jnp.where(lane <= first + sub, kept, 0.0))
        if p + 1 < count:
            rows[p + 1] = moved
        for i in range(p + 2, count):
            col = columns[i - p - 1]
            terms = [col[t] * solved[t] for t in range(PANEL)]
            while len(terms) > 1:
                terms = [a + b for a, b in zip(terms[::2], terms[1::2])]
            rows[i] = jnp.where(inside, 0.0, rows[i]) - terms[0]
    return result


def factor_step(work, j):
    blocks = work.shape[0] // BLOCK
    at = slice(j * BLOCK, (j + 1) * BLOCK)
    diagonal = work[at, at]
    inverse = jnp.concatenate(
        diagonal_inverse([diagonal[PANEL * i : PANEL * (i + 1), :] for i in range(BLOCK // PANEL)]), axis=0
    )
    pair = split_bf16(inverse)
    work[at, at] = identity(BLOCK)
    scaled = dot3(pair, split_bf16(work[at, :]), ((1,), (0,)))
    work[at, :] = scaled
    if j + 1 == blocks:
        return
    scaled_pair = split_bf16(scaled)
    below = slice((j + 1) * BLOCK, blocks * BLOCK)
    left = dot3(split_bf16(work[below, at]), pair, ((1,), (1,)))
    work[below, at] = jnp.zeros((left.shape[0], BLOCK), jnp.float32)
    work[below, :] = work[below, :] - dot3(split_bf16(left), scaled_pair, ((1,), (0,)))


def factor_in_place(work):
    for j in range(work.shape[0] // BLOCK):
        factor_step(work, j)


def identity(size):
    return (
        lax.broadcasted_iota(jnp.int32, (size, size), 0) == lax.broadcasted_iota(jnp.int32, (size, size), 1)
    ).astype(jnp.float32)


def block_lower(value):
    row = lax.broadcasted_iota(jnp.int32, value.shape, 0) // BLOCK
    column = lax.broadcasted_iota(jnp.int32, value.shape, 1) // BLOCK
    return jnp.where(column <= row, value, 0.0)


def load_symmetric(tiles, scale, ridge, work):
    side = tiles[0].shape[0]
    diagonal = ridge * identity(side)
    low, high = slice(0, side), slice(side, 2 * side)
    work[low, low] = tiles[0][...] * scale + diagonal
    work[high, high] = tiles[1][...] * scale + diagonal
    cross = tiles[2][...] * scale
    work[high, low] = cross
    work[low, high] = cross.T


def first_kernel(scale, ridge, tiles_ref, out_ref):
    load_symmetric([tiles_ref.at[i] for i in range(3)], scale, ridge, out_ref)
    factor_step(out_ref, 0)


def later_kernel(j, work_ref, out_ref):
    out_ref[...] = work_ref[...]
    factor_step(out_ref, j)
    if (j + 1) * BLOCK == out_ref.shape[0]:
        out_ref[...] = block_lower(out_ref[...])


def second_kernel(scale, ridge, first_ref, tiles_ref, out_ref, work, under):
    half = first_ref.shape[0]
    side = half // 2
    load_symmetric([tiles_ref.at[4 + i] for i in range(3)], scale, ridge, work)
    first = split_bf16(first_ref[...])
    for i in range(2):
        rows = slice(i * side, (i + 1) * side)
        cross = jnp.concatenate([tiles_ref[2 * i], tiles_ref[2 * i + 1]], axis=1) * scale
        under[rows, :] = dot3(split_bf16(cross), first, ((1,), (1,)))
    pair = split_bf16(under[...])
    for i in range(2):
        rows = slice(i * side, (i + 1) * side)
        mine = tuple(part[rows, :] for part in pair)
        work[rows, :] = work[rows, :] - dot3(mine, pair, ((1,), (1,)))
    under[...] = dot3(pair, first, ((1,), (0,)))
    factor_in_place(work)
    second = block_lower(work[...])
    out_ref[:half, :half] = first_ref[...].astype(out_ref.dtype)
    out_ref[:half, half:] = jnp.zeros((half, half), out_ref.dtype)
    out_ref[half:, :half] = (-dot3(split_bf16(second), split_bf16(under[...]), ((1,), (0,)))).astype(out_ref.dtype)
    out_ref[half:, half:] = second.astype(out_ref.dtype)


def kernel_call(kernel, out, operands, scratch, cost):
    whole = pl.BlockSpec(memory_space=pltpu.VMEM)
    return pl.pallas_call(
        kernel,
        out_shape=out,
        in_specs=[whole] * len(operands),
        out_specs=whole,
        scratch_shapes=scratch,
        compiler_params=pltpu.CompilerParams(vmem_limit_bytes=40 * 1024 * 1024),
        cost_estimate=pl.CostEstimate(flops=cost, bytes_accessed=4 << 20, transcendentals=0),
    )(*operands)


CHAIN_FLOPS = 10_000_000


def inverse_first(tiles, scale, ridge):
    half = 2 * tiles.shape[-1]
    shape = jax.ShapeDtypeStruct((half, half), jnp.float32)
    steps = half // BLOCK
    stages = [
        kernel_call(functools.partial(first_kernel, scale, ridge), shape, (tiles,), [], CHAIN_FLOPS // steps)
    ]
    for j in range(1, steps):
        stages.append(
            kernel_call(functools.partial(later_kernel, j), shape, (stages[-1],), [], CHAIN_FLOPS // steps)
        )
    return stages


def inverse_second(first, tiles, scale, ridge):
    half = first.shape[0]
    square = pltpu.VMEM((half, half), jnp.float32)
    return kernel_call(
        functools.partial(second_kernel, scale, ridge),
        jax.ShapeDtypeStruct((2 * half, 2 * half), jnp.bfloat16),
        (first, tiles),
        [square, square],
        CHAIN_FLOPS,
    )


FIRST_TILES = ((0, 0), (1, 1), (1, 0))
SECOND_TILES = ((2, 0), (2, 1), (3, 0), (3, 1), (2, 2), (3, 3), (3, 2))


def gram_kernel(rows_ref, columns_ref, left_ref, right_ref, out_ref):
    out_ref[0] = lax.dot_general(
        left_ref[...], right_ref[...], (((0,), (0,)), ((), ())), preferred_element_type=jnp.float32
    )


def gram_tiles(values, tiles):
    count, width = values.shape
    side = width // 4
    rows = jnp.array([tile[0] for tile in tiles], jnp.int32)
    columns = jnp.array([tile[1] for tile in tiles], jnp.int32)
    return pl.pallas_call(
        gram_kernel,
        grid_spec=pltpu.PrefetchScalarGridSpec(
            num_scalar_prefetch=2,
            grid=(len(tiles),),
            in_specs=[
                pl.BlockSpec((count, side), lambda i, row, column: (0, row[i])),
                pl.BlockSpec((count, side), lambda i, row, column: (0, column[i])),
            ],
            out_specs=pl.BlockSpec((1, side, side), lambda i, row, column: (i, 0, 0)),
        ),
        out_shape=jax.ShapeDtypeStruct((len(tiles), side, side), jnp.float32),
        compiler_params=pltpu.CompilerParams(vmem_limit_bytes=24 * 1024 * 1024),
        cost_estimate=pl.CostEstimate(
            flops=2 * len(tiles) * count * side * side, bytes_accessed=4 << 20, transcendentals=0
        ),
    )(rows, columns, values, values)


def halve(part, bit, start=(), beside=()):
    halves = part.reshape(2, -1, part.shape[-1])
    high = (lax.axis_index("dp") // bit) % 2
    kept = lax.dynamic_index_in_dim(halves, high, 0, False)
    sent = after(lax.dynamic_index_in_dim(halves, 1 - high, 0, False), *start)
    return kept + after(exchange(sent, "dp", bit), *beside)


def rejoin(part, bit, *beside):
    return ordered(part, "dp", bit, *beside).reshape(-1, part.shape[-1])


def sum_both(first, second):
    bits = bits_of(lax.axis_size("dp"), 1)[::-1]
    near, far = bits[:-2], bits[-2:]
    first = halve(first, near[0])
    second_sent = after(second, first)
    for bit in near[1:]:
        first = halve(first, bit)
    second = halve(second_sent, bits[0], (), (first,))
    first = first + after(exchange(first, "dp", far[0]), second)
    second_next = functools.partial(halve, second, bits[1])
    first = first + exchange(first, "dp", far[1])
    second = second_next((), (first,))
    first = rejoin(first, near[-1], second)
    for bit in near[:-1][::-1]:
        first = rejoin(first, bit)

    def rest(besides, outgoing):
        part, at = second, 0
        for bit in bits[2:]:
            part = halve(part, bit, (), besides[at : at + 1])
            at += 1
        for bit in bits[::-1]:
            part = rejoin(part, bit, *besides[at : at + 1])
            if bit == 2:
                outgoing = after(outgoing, part)
            at += 1
        return part, outgoing

    return first, rest


def filing_kernel(rows_ref, inverse_ref, centroids_ref, out_ref):
    count, _, slots, width = rows_ref.shape
    rows = rows_ref[...].reshape(count * slots, width)
    whitened = lax.dot_general(rows, inverse_ref[...], (((1,), (1,)), ((), ())), preferred_element_type=jnp.float32)
    residual = whitened - centroids_ref[0].astype(jnp.float32)
    out_ref[0] = jnp.where(rows[:, :1].astype(jnp.float32) < EMPTY, residual, 0.0).astype(out_ref.dtype)


def file_rows(incoming, inverse, centroids):
    count, lists, slots, width = incoming.shape
    return pl.pallas_call(
        filing_kernel,
        grid=(lists,),
        in_specs=[
            pl.BlockSpec((count, 1, slots, width), lambda i: (0, i, 0, 0)),
            pl.BlockSpec((width, width), lambda i: (0, 0)),
            pl.BlockSpec((1, 1, width), lambda i: (i, 0, 0)),
        ],
        out_specs=pl.BlockSpec((1, count * slots, width), lambda i: (i, 0, 0)),
        out_shape=jax.ShapeDtypeStruct((lists, count * slots, width), jnp.bfloat16),
        compiler_params=pltpu.CompilerParams(vmem_limit_bytes=24 * 1024 * 1024),
    )(incoming, inverse, centroids[:, None, :])


EMPTY = 64.0


def slots_of(assigned, owner_map, lists_owned, slot_count):
    row_count = assigned.shape[0]
    choose = assigned[:, None] == jnp.arange(owner_map.shape[0], dtype=jnp.int32)[None, :]
    position = jnp.sum(jnp.where(choose, owner_map[None, :], 0), axis=1)
    order = jnp.arange(row_count, dtype=jnp.int32)
    earlier = (assigned[:, None] == assigned[None, :]) & (order[:, None] > order[None, :])
    rank = jnp.sum(earlier.astype(jnp.int32), axis=1)
    return position * slot_count + rank


def place_rows(rows, slot_index, slot_total):
    chosen = jnp.arange(slot_total, dtype=jnp.int32)[:, None] == slot_index[None, :]
    placed = jnp.dot(chosen.astype(jnp.bfloat16), rows, preferred_element_type=jnp.float32)
    return jnp.where(jnp.any(chosen, axis=1, keepdims=True), placed, EMPTY).astype(jnp.bfloat16)


def body(
    tokens,
    lengths,
    input_weight,
    output_weight,
    norm_gain,
    expand_weight,
    shrink_weight,
    assigned,
    owner_map,
    centroids,
):
    row_count, model_width = tokens.shape
    device_count = lax.axis_size("dp")
    nt = functools.partial(
        lax.dot_general, dimension_numbers=(((1,), (1,)), ((), ())), preferred_element_type=jnp.float32
    )
    middle = jnp.concatenate([output_weight.T, expand_weight.T], axis=0)
    far_bits = bits_of(device_count, 4)
    near, far = far_bits[1:], far_bits[:1]
    input_part = gather_far(gather_far(own_share(input_weight.T), far), near)
    middle_part = gather_far(after(own_share(middle), input_part), far)
    input_first = near_first(input_part)
    middle_part = gather_far(middle_part, near, *input_first)
    shrink_part = gather_far(after(own_share(shrink_weight.T), middle_part), far)
    input_part = near_rest(*input_first)
    middle_first = near_first(middle_part, *input_part)
    shrink_part = gather_far(shrink_part, near, *input_part)
    projected = nt(gather_cores(*input_part), tokens).astype(jnp.bfloat16)
    attended = attend(after(projected, *middle_first), segment_ids(lengths[0], row_count))
    middle_part = near_rest(*middle_first, attended)
    shrink_first = near_first(after(shrink_part, *middle_first), attended)
    middle_rows = gather_cores(*middle_part).reshape(device_count, -1, model_width)
    own_output = output_weight.shape[1]
    output_rows = middle_rows[:, :own_output].reshape(-1, model_width)
    expand_rows = middle_rows[:, own_output:].reshape(-1, model_width)
    mixed_out = lax.dot_general(
        attended, output_rows, (((0,), (1,)), ((), ())), preferred_element_type=jnp.float32
    )
    first_norm = layer_norm(tokens.astype(jnp.float32) + mixed_out, norm_gain).astype(jnp.bfloat16)
    expanded = expand(after(first_norm, *shrink_first), expand_rows)
    shrink_part = near_rest(*shrink_first, expanded)
    shrink_rows = gather_cores(*shrink_part)
    reduced = nt(expanded, shrink_rows)
    embedded = layer_norm(first_norm.astype(jnp.float32) + reduced, 1.0).astype(jnp.bfloat16)
    lists_owned = centroids.shape[0]
    list_total = lists_owned * device_count
    slot_count = max(2, 2 * row_count // list_total)
    slot_index = slots_of(assigned, owner_map, lists_owned, slot_count)
    outgoing = place_rows(embedded, slot_index, list_total * slot_count)
    scale = 1.0 / (row_count * device_count)
    first_tiles = gram_tiles(embedded, FIRST_TILES)
    second_tiles = gram_tiles(after(embedded, first_tiles), SECOND_TILES)
    flat = functools.partial(jnp.reshape, shape=(-1, first_tiles.shape[-1]))
    first_sum, rest = sum_both(flat(first_tiles), flat(second_tiles))
    stages = inverse_first(first_sum.reshape(first_tiles.shape), scale, ridge_term)
    second_sum, outgoing = rest(stages, outgoing)
    second_sum = second_sum.reshape(second_tiles.shape)
    first = stages[-1]
    incoming = lax.all_to_all(
        outgoing.reshape(device_count, lists_owned, slot_count, model_width),
        "dp",
        split_axis=0,
        concat_axis=0,
        tiled=True,
    )
    inverse = inverse_second(first, second_sum, scale, ridge_term)
    if slot_count % 16 == 0:
        return file_rows(incoming, inverse, centroids)
    arrived = incoming.transpose(1, 0, 2, 3).reshape(-1, model_width)
    whitened = lax.dot_general(
        arrived, inverse, (((1,), (1,)), ((), ())), preferred_element_type=jnp.float32
    ).reshape(lists_owned, device_count * slot_count, model_width)
    occupied = arrived[:, :1].reshape(lists_owned, device_count * slot_count, 1) < EMPTY
    residual = whitened - centroids.astype(jnp.float32)[:, None, :]
    return jnp.where(occupied, residual, 0.0).astype(jnp.bfloat16)


def solution(mesh):
    in_specs = (
        P(("groups", "dp"), None),
        P(("groups", "dp"), None),
        P(None, "dp"),
        P(None, "dp"),
        P(),
        P(None, "dp"),
        P(None, "dp"),
        P(("groups", "dp")),
        P("groups"),
        P("dp", None),
    )
    out_specs = P(("groups", "dp"), None, None)
    return jax.shard_map(body, mesh=mesh, in_specs=in_specs, out_specs=out_specs, check_vma=False)
```
